128 devices in a mesh: pitch: 8 (over y, core), span: 16 (over x, z).
Axes of the slice: x: 4, y: 4, z: 4, core: 2. Of those that a mesh axis runs over, the one named last changes fastest.
Arguments:
- flow_state: float32 [4, 256, 1024, 256], P(None, 'pitch', 'span'), may hold values from -6 to 6
- wall_inverse: float32 [64, 64], replicated, as said below
- metal_inverse: float32 [16, 16], replicated, as said below
- metal_state: float32 [16, 262144], P(None, ('pitch', 'span')), may hold values from -6 to 6
- metal_conduct: float32 [262144], P(('pitch', 'span')), may hold values from 0.3 to 3
- face_coef: float32 [2, 131072], P(None, ('pitch', 'span')), may hold values from 0.3 to 3
- owner_map: int32 [131072, 1], P(('pitch', 'span')), may hold values from 0 to 127; in each aligned block of 1024 rows (0 to 1023, 1024 to 2047, ...) at most 16 rows name the same one
- face_cell: int32 [131072], P(('pitch', 'span')), may hold values from 0 to 2047
- sample_col: int32 [131072], P(('pitch', 'span')), may hold values from 0 to 2047
- sample_low: int32 [131072], P(('pitch', 'span')), may hold values from 0 to 192
Outputs:
- new_state: float32 [4, 256, 1024, 256], P(None, 'pitch', 'span')
- metal_out: float32 [16, 262144], P(None, ('pitch', 'span'))
The draws below stay inside these ranges and needn't reach their ends.
Inputs may be any that keep to these rules, and one draw needn't show every extreme that they name: `owner_map`: at most 16 faces of one device have the same owner; in every draw some device sends exactly 16 faces to one owner. `face_cell`: columns are numbered pitch cell times 64 plus span cell. `sample_col`: numbered as face_cell. `wall_inverse`: diagonal entries are the largest of their rows, within 0.5 to 1. `metal_inverse`: diagonal entries are the largest of their rows, within 0.5 to 1.
All inputs are finite; a program needn't handle non-finite values.
Results may differ from the reference program's by a relative error of at most 0.0001.
Values sent between devices are 32-bit elements; how exact they have to be, the bound alone decides.
No kernel may reach another device: no remote copies, remote signals or barrier semaphores. Data moves between devices by JAX's collectives and lax.ppermute only.
A program may use at most 128 MiB of HBM per device.

```python
import math
import jax
import jax.numpy as jnp
import numpy as np
from jax import lax

CP = 32
CS = 64
GN = 256
F_DEV = 1024
WM = 64
MP = 16
PICARD = 3
CAP = 16
SLOT_DEV = 2048
SLOTS = 262144
F_TOTAL = 131072
NP = 256
NS = 1024
N_SPAN = 16
DEVICES = 128


def inverse_table(key, order):
    key_diag = jax.random.fold_in(key, 11)
    key_off = jax.random.fold_in(key, 23)
    diagonal = jax.random.uniform(key_diag, (order,), jnp.float32, 0.5, 1.0)
    spread = 0.5 / order ** 0.5
    offdiag = jax.random.normal(key_off, (order, order), jnp.float32) * spread
    rows = jnp.arange(order)[:, None]
    cols = jnp.arange(order)[None, :]
    identity = (rows == cols).astype(jnp.float32)
    offdiag = jnp.clip(offdiag, -0.45, 0.45) * (1.0 - identity)
    return identity * diagonal[:, None] + offdiag


def draw_wall_inverse(key, part):
    return inverse_table(jax.random.fold_in(key, 101), WM)


def draw_metal_inverse(key, part):
    return inverse_table(jax.random.fold_in(key, 202), MP)


def place_ends(values, stream_key, low, high):
    index_at = [jax.random.randint(jax.random.fold_in(stream_key, axis), (), 0, length) for axis, length in enumerate(values.shape)]
    main_axis = values.shape.index(max(values.shape))
    next_to = index_at[:main_axis] + [(index_at[main_axis] + 1) % values.shape[main_axis]] + index_at[main_axis + 1:]
    return values.at[tuple(index_at)].set(low).at[tuple(next_to)].set(high)


def shard_levels(rng, dims, cuts, smallest, largest):
    def one(position, blocks):
        draws = jax.random.uniform(jax.random.fold_in(jax.random.fold_in(rng, 6), position), (blocks,), jnp.float32, smallest / len(cuts), largest / len(cuts))
        return jnp.repeat(jnp.exp(draws), dims[position] // blocks).reshape((-1,) + (1,) * (len(dims) - position - 1))

    gain = one(*cuts[0])
    for cut in cuts[1:]:
        gain = gain * one(*cut)
    return gain


def deal_out(rng, own, number, rows, count, top, reach, slope):
    ranking = jax.random.permutation(rng, count)
    heavy_load, common = portions_of(count, rows * top, reach, slope, True), portions_of(count, rows * top, reach, slope, False)
    places = jnp.arange(count)

    def named(lengths, turn):
        used = int((lengths > 0).sum())
        fixed = max(1, used // 4)
        shifted = fixed + (places - fixed + turn * (used - fixed)) % max(1, count - fixed)
        return jnp.zeros((count,), jnp.int32).at[ranking[jnp.where(places < fixed, places, shifted)]].set(jnp.asarray(lengths, jnp.int32))

    lengths = jnp.where(number % 4 == 0, named(heavy_load, number // 4), named(common, number - number // 4 - 1))
    mixed = jax.random.permutation(jax.random.fold_in(own, 3), count)
    source_of, sink = mixed[0:count // 2 * 2:2], mixed[1:count // 2 * 2:2]
    slack = jnp.minimum(lengths[source_of] - 1, reach - lengths[sink]) // 2
    slack = jnp.where((source_of == ranking[0]) | (sink == ranking[0]) | (lengths[sink] == 0), 0, jnp.maximum(slack, 0))
    shifted = jax.random.randint(jax.random.fold_in(own, 4), (count // 2,), 0, 1 << 20) % (slack + 1)
    lengths = lengths.at[source_of].add(-shifted).at[sink].add(shifted)
    labels = jnp.searchsorted(jnp.cumsum(lengths), jnp.arange(rows * top), side="right").astype(jnp.int32)
    listing = labels.reshape(top, rows).T
    listing = listing[jax.random.permutation(jax.random.fold_in(own, 1), rows)]
    turn = jax.random.randint(jax.random.fold_in(own, 2), (rows, 1), 0, top)
    return jnp.take_along_axis(listing, (jnp.arange(top)[None, :] + turn) % top, axis=1)


def portions_of(count, total, reach, skew, full):
    portions = [(1 << 20) // math.isqrt(standing ** skew) + 1 for standing in range(1, count + 1)]
    largest = reach if full else min(reach, max(-(-total // count), total * portions[0] // sum(portions)))
    least = 1 if total - largest >= count - 1 else 0
    given, spare = [largest] + [least] * (count - 1), total - largest - least * (count - 1)
    while spare > 0:
        movable = [i for i in range(1, count) if given[i] < largest] or [i for i in range(1, count) if given[i] < reach]
        pool, budget = sum([portions[i] for i in movable]), spare
        for i in movable:
            extra = min(reach - given[i], max(1, budget * portions[i] // pool), spare)
            given[i] = given[i] + extra
            spare = spare - extra
    return np.array(given)


def bell_draw(own_key, dims, scale, bound, cuts=(), kind=jnp.bfloat16):
    drawn = scale * jax.random.normal(own_key, dims, jnp.float32)
    if cuts:
        drawn = drawn * shard_levels(own_key, dims, cuts, -0.22, 0.18)
    return jnp.clip(drawn, -bound, bound).astype(kind)


def setup_inputs(seed: int = 0) -> dict:
    key_of = jax.random.split(jax.random.key(seed), 11)
    flow_state = bell_draw(key_of[0], (4, NP, NS, GN), 1.0, 6.0, ((1, 8), (2, 16)), jnp.float32)
    wall_inverse = draw_wall_inverse(jax.random.fold_in(key_of[10], 71), 0)
    metal_inverse = draw_metal_inverse(jax.random.fold_in(key_of[10], 71), 0)
    metal_state = bell_draw(key_of[3], (MP, SLOTS), 1.0, 6.0, ((1, 128),), jnp.float32)
    metal_conduct = jnp.clip(jnp.exp(math.log(3.0) - 2.3025851 * jax.random.uniform(key_of[4], (SLOTS,), jnp.float32) ** shard_levels(key_of[4], (SLOTS,), ((0, 128),), -0.2, 0.2)), 0.3, 3.0)
    face_coef = jnp.clip(jnp.exp(math.log(3.0) - 2.3025851 * jax.random.uniform(key_of[5], (2, F_TOTAL), jnp.float32) ** shard_levels(key_of[5], (2, F_TOTAL), ((1, 128),), -0.2, 0.2)), 0.3, 3.0)
    owner_map_keys = jax.random.split(jax.random.fold_in(key_of[6], 1), F_TOTAL // F_DEV)
    owner_map_turns = jax.random.permutation(jax.random.fold_in(key_of[6], 3), F_TOTAL // F_DEV)
    owner_map = jax.vmap(lambda own, number: deal_out(jax.random.fold_in(key_of[6], 2), own, number, F_DEV, DEVICES, 1, CAP, 1))(owner_map_keys, owner_map_turns).reshape((F_TOTAL, 1))
    face_cell = place_ends(jax.random.randint(key_of[7], (F_TOTAL,), 0, CP * CS), jax.random.fold_in(key_of[7], 1), 0, (CP * CS) - 1).astype(jnp.int32)
    sample_col = place_ends(jax.random.randint(key_of[8], (F_TOTAL,), 0, CP * CS), jax.random.fold_in(key_of[8], 1), 0, (CP * CS) - 1).astype(jnp.int32)
    sample_low = place_ends(jax.random.randint(key_of[9], (F_TOTAL,), 0, GN - WM + 1), jax.random.fold_in(key_of[9], 1), 0, GN - WM).astype(jnp.int32)
    return {"flow_state": flow_state, "wall_inverse": wall_inverse, "metal_inverse": metal_inverse, "metal_state": metal_state, "metal_conduct": metal_conduct, "face_coef": face_coef, "owner_map": owner_map, "face_cell": face_cell, "sample_col": sample_col, "sample_low": sample_low}


PRECISE = lax.Precision.HIGHEST
ALPHA_FLUID = 0.5
BETA_METAL = 0.5
DRAG_COEF = 0.5
TIME_STEP = 0.5
DIFFUSION = 0.2
ADVECTION = 0.6
WALL_AREA = 1.0

def wall_columns(packed, conduct_fluid, viscosity, metal_old, conduct_metal, occupied, wall_inverse, metal_inverse):
    slot_count = packed.shape[1]
    profiles = packed.reshape(3, WM, slot_count)
    force_u = profiles[0]
    force_w = profiles[1]
    force_t = profiles[2]
    speed_u = jnp.dot(wall_inverse, force_u, precision=PRECISE)
    speed_w = jnp.dot(wall_inverse, force_w, precision=PRECISE)
    for picard_step in range(PICARD):
        damping = DRAG_COEF / jnp.sqrt(1.0 + speed_u * speed_u + speed_w * speed_w)
        next_u = jnp.dot(wall_inverse, force_u - damping * speed_u, precision=PRECISE)
        next_w = jnp.dot(wall_inverse, force_w - damping * speed_w, precision=PRECISE)
        speed_u = next_u
        speed_w = next_w
    fluid_top = jnp.dot(wall_inverse[0], force_t, precision=PRECISE)
    metal_free = jnp.dot(metal_inverse, metal_old, precision=PRECISE)
    corner_fluid = wall_inverse[0, 0]
    corner_metal = metal_inverse[0, 0]
    denominator = conduct_fluid * (1.0 - ALPHA_FLUID * corner_fluid) + conduct_metal * (1.0 - BETA_METAL * corner_metal) + (1.0 - occupied)
    wall_temp = (conduct_fluid * fluid_top + conduct_metal * metal_free[0]) / denominator
    heat_flux = conduct_fluid * (fluid_top + (ALPHA_FLUID * corner_fluid - 1.0) * wall_temp)
    metal_new = metal_free + BETA_METAL * wall_temp[None, :] * metal_inverse[:, 0:1]
    fluxes = jnp.stack([viscosity * speed_u[0], viscosity * speed_w[0], heat_flux])
    return (fluxes, metal_new)

def advance(current, pitch_next, pitch_prev, span_next, span_prev, wall_source):
    normal_pad = jnp.pad(current, ((0, 0), (0, 0), (0, 0), (1, 1)), mode='edge')
    laplace = pitch_next + pitch_prev + span_next + span_prev + normal_pad[..., 2:] + normal_pad[..., :-2] - 6.0 * current
    tendency = DIFFUSION * laplace - ADVECTION * 0.5 * (pitch_next - pitch_prev)
    tendency = tendency.at[:3, :, :, 0].add(wall_source)
    return current + TIME_STEP * tendency

def reference(flow_state, wall_inverse, metal_inverse, metal_state, metal_conduct, face_coef, owner_map, face_cell, sample_col, sample_low):
    home_dev = jnp.arange(F_TOTAL, dtype=jnp.int32) // F_DEV
    target = owner_map[:, 0]
    choose = (target.reshape(DEVICES, F_DEV, 1) == jnp.arange(DEVICES, dtype=jnp.int32)[None, None, :]).astype(jnp.int32)
    before = lax.optimization_barrier(jnp.sum((jnp.cumsum(choose, axis=1) - choose) * choose, axis=2)).reshape(F_TOTAL)
    slot_global = target * SLOT_DEV + home_dev * CAP + before
    pitch_home = home_dev // N_SPAN
    span_home = home_dev % N_SPAN
    row_pitch = pitch_home * CP + sample_col // CS
    row_span = span_home * CS + sample_col % CS
    window = sample_low[:, None] + jnp.arange(WM, dtype=jnp.int32)[None, :]
    samples = flow_state[:3][:, row_pitch[:, None], row_span[:, None], window]
    packed = jnp.transpose(samples, (0, 2, 1)).reshape(3 * WM, F_TOTAL)
    occupied = jnp.ones((F_TOTAL,), jnp.float32)
    fluxes, metal_new = wall_columns(packed, face_coef[0], face_coef[1], metal_state[:, slot_global], metal_conduct[slot_global], occupied, wall_inverse, metal_inverse)
    metal_out = metal_state.at[:, slot_global].set(metal_new)
    cell_pitch = pitch_home * CP + face_cell // CS
    cell_span = span_home * CS + face_cell % CS
    column = cell_pitch * NS + cell_span
    summed = jax.ops.segment_sum(fluxes.T, column, num_segments=NP * NS)
    wall_source = -WALL_AREA * summed.T.reshape(3, NP, NS)
    pitch_next = jnp.roll(flow_state, -1, axis=1)
    pitch_prev = jnp.roll(flow_state, 1, axis=1)
    span_pad = jnp.pad(flow_state, ((0, 0), (0, 0), (1, 1), (0, 0)))
    new_state = advance(flow_state, pitch_next, pitch_prev, span_pad[:, :, 2:], span_pad[:, :, :-2], wall_source)
    return (new_state, metal_out)
```

```python
import jax
import jax.numpy as jnp
from jax import lax
from jax.experimental import pallas as pl
from jax.experimental.pallas import tpu as pltpu
from jax.sharding import PartitionSpec as P

CP = 32
CS = 64
GN = 256
WM = 64
MP = 16
CAP = 16
DEV = 128
FACES = 1024
SLOT_DEV = 2048
COLS = CP * CS
PICARD = 3

F32 = jnp.float32
BF16 = jnp.bfloat16
I32 = jnp.int32
AXES = ("pitch", "span")
VMEM_LIMIT = 48 * 1024 * 1024
VMEM_WHOLE = 60 * 1024 * 1024
FB = 256
PAD = 8


def iota(shape, dim):
    return lax.broadcasted_iota(I32, shape, dim)


def dot_nn(a, b):
    return lax.dot_general(a, b, (((1,), (0,)), ((), ())), preferred_element_type=F32)


def dot_nt(a, b):
    return lax.dot_general(a, b, (((1,), (1,)), ((), ())), preferred_element_type=F32)


def split2(x):
    hi = x.astype(BF16).astype(F32)
    return hi, x - hi


def split3(x):
    hi = x.astype(BF16).astype(F32)
    rest = x - hi
    mid = rest.astype(BF16).astype(F32)
    return hi, mid, rest - mid


def cast(x):
    return x.astype(BF16)


def cell_tables(cell_row):
    width = cell_row.shape[1]
    span_hot = iota((CS, width), 0) == (cell_row & (CS - 1))
    pitch_hot = iota((CP, width), 0) == (cell_row >> 6)
    return jnp.where(span_hot, 1.0, 0.0), pitch_hot


def gather_lane(source, index):
    return jnp.take_along_axis(source, index, axis=1)


def pick_rows(refs, col_ref, base):
    sub = iota((8, 128), 0)
    blocks = [None] * len(refs)
    for i in range(8):
        at = col_ref[base + i]
        for k, ref in enumerate(refs):
            row = jnp.broadcast_to(ref[pl.ds(at, 1), :], (8, 128))
            blocks[k] = row if i == 0 else jnp.where(sub == i, row, blocks[k])
    return blocks


def first_kernel(
    state, *args,
):
    sources, (send, first_p, last_p, first_s, last_s, rank, top, free, walls) = args[:9], args[9:18]
    cur, lowb, temp, force, out_send, edge_p, edge_s, sems, *held = args[18:]
    col, low, owner, coef, cell, wall_inv, metal_inv, metal, conduct = held
    small = [
        pltpu.make_async_copy(source, target, sems.at[9 + (i == 0)])
        for i, (source, target) in enumerate(zip(sources, held))
    ]
    for copy in small:
        copy.start()
    columns = state.reshape(4, COLS, GN)
    loads = []
    for i, c in enumerate((2, 0, 1, 3)):
        for h in range(2):
            loads.append(
                pltpu.make_async_copy(
                    columns.at[c, :, pl.ds(128 * h, 128)],
                    cur.at[2 * c + h, pl.ds(0, COLS)],
                    sems.at[i],
                )
            )
    for copy in loads:
        copy.start()
    edges_in = [
        pltpu.make_async_copy(state.at[:, 0], edge_p.at[0], sems.at[4]),
        pltpu.make_async_copy(state.at[:, CP - 1], edge_p.at[1], sems.at[5]),
    ]
    for copy in edges_in:
        copy.start()

    for copy in small[1:]:
        copy.wait()

    eye = iota((128, 128), 0) == iota((128, 128), 1)
    ones = jnp.ones((128, 128), BF16)
    low_f = low[...].astype(F32)
    for b in range(FACES // 128):
        diag = jnp.where(eye, low_f[:, 128 * b : 128 * (b + 1)], 0.0)
        lowb[pl.ds(128 * b, 128), :] = dot_nn(cast(diag), ones).astype(I32)

    m = metal[...]
    inv = metal_inv[...]
    v = inv[:, 0:1] * m[0:1, :]
    for j in range(1, MP):
        v = v + inv[:, j : j + 1] * m[j : j + 1, :]
    free[...] = v
    v0 = jnp.concatenate([v[0:1, 128 * g : 128 * (g + 1)] for g in range(16)], axis=0)
    spread = jnp.where((iota((DEV, 16), 0) >> 3) == iota((DEV, 16), 1), 1.0, 0.0)
    parts = jnp.concatenate(split3(v0) + split3(conduct[...]), axis=1)
    wide = dot_nn(cast(spread), cast(parts))
    lane = iota((DEV, 128), 1)
    mine = (lane >> 4) == (iota((DEV, 128), 0) & 7)
    folded = []
    for k in range(2):
        a = wide[:, 384 * k : 384 * (k + 1)]
        y = jnp.where(mine, a[:, 0:128] + a[:, 128:256] + a[:, 256:384], 0.0)
        for step in (64, 32, 16):
            y = y + pltpu.roll(y, step, 1)
        folded.append(y)
    own_half = jnp.where(lane < 16, folded[0], folded[1])

    before = jnp.where(iota((FB, FB), 0) < iota((FB, FB), 1), 1.0, 0.0).astype(BF16)
    carry = jnp.zeros((DEV, 1), F32)
    for b in range(FACES // FB):
        cols = slice(FB * b, FB * (b + 1))
        hot = jnp.where(iota((DEV, FB), 0) == owner[:, cols], 1.0, 0.0)
        prior = dot_nn(cast(hot), before) + carry
        carry = carry + jnp.sum(hot, axis=1, keepdims=True)
        rank[:, cols] = jnp.sum(hot * prior, axis=0, keepdims=True).astype(I32)

    for copy in edges_in:
        copy.wait()
    edges_out = [
        pltpu.make_async_copy(edge_p.at[0], first_p, sems.at[4]),
        pltpu.make_async_copy(edge_p.at[1], last_p, sems.at[5]),
    ]
    for copy in edges_out:
        copy.start()
    small[0].wait()
    for copy in loads[0:6]:
        copy.wait()
    halves = [[cur.at[2 * c + h] for h in range(2)] for c in range(4)]
    lane8 = iota((8, 128), 1)
    left = lane8 < WM

    def body(g, _):
        base = g * 8
        index = lowb[pl.ds(base, 8), :] + (lane8 & (WM - 1))
        near = index < 128
        index = index & 127
        found = pick_rows([halves[c][h] for c in range(3) for h in range(2)], col, base)
        found = [gather_lane(x, index) for x in found]
        picked = [jnp.where(near, found[2 * c], found[2 * c + 1]) for c in range(3)]
        force[pl.ds(base, 8), :] = jnp.where(left, picked[0], picked[1])
        temp[pl.ds(base, 8), :] = picked[2]
        return 0

    lax.fori_loop(0, FACES // 8, body, 0, unroll=8)

    g = wall_inv[...]
    g_hi, g_lo = split2(g)
    top_hi, top_lo = g_hi[0:1, :], g_lo[0:1, :]
    none = jnp.zeros((1, WM), F32)
    row16 = iota((16, 128), 0)
    query = jnp.where(
        row16 == 0,
        jnp.concatenate([top_hi, top_hi], axis=1),
        jnp.where(row16 == 1, jnp.concatenate([top_lo, none], axis=1), 0.0),
    )
    total = jnp.zeros((DEV, 128), F32)
    left_b = iota((FB, 128), 1) < WM
    for b in range(FACES // FB):
        cols = slice(FB * b, FB * (b + 1))
        x_hi, x_lo = split2(temp[cols, :])
        p = dot_nt(cast(query), cast(jnp.where(left_b, x_hi, x_lo)))
        p = p[0:1, :] + p[1:2, :]
        top[:, cols] = p
        hot = jnp.where(iota((DEV, FB), 0) == owner[:, cols], 1.0, 0.0)
        which = iota((CAP, FB), 0) == rank[:, cols]
        kf_parts = split3(coef[0:1, cols])
        p_parts = split3(p)
        pieces = [jnp.zeros((32, FB), F32)]
        for kf_part, p_part in zip(kf_parts, p_parts):
            pieces.append(jnp.where(which, kf_part, 0.0))
            pieces.append(jnp.where(which, p_part, 0.0))
        total = total + dot_nt(cast(hot), cast(jnp.concatenate(pieces, axis=0)))
    total = total + pltpu.roll(total, 96, 1) + pltpu.roll(total, 64, 1)
    out_send[...] = jnp.where(lane < 32, own_half, jnp.where(lane < 64, total, 0.0))
    give = [pltpu.make_async_copy(out_send, send, sems.at[6])]
    give[0].start()

    for copy in loads[6:]:
        copy.wait()
    for c in range(4):
        for h in range(2):
            lanes = slice(128 * h, 128 * h + 128)
            for p in range(0, CP, 8):
                edge_s[0, c, p : p + 8, lanes] = halves[c][h][pl.ds(p * CS, 8, stride=CS), :]
                edge_s[1, c, p : p + 8, lanes] = halves[c][h][
                    pl.ds(p * CS + CS - 1, 8, stride=CS), :
                ]
    give.append(pltpu.make_async_copy(edge_s.at[0], first_s, sems.at[7]))
    give.append(pltpu.make_async_copy(edge_s.at[1], last_s, sems.at[8]))
    give[1].start()
    give[2].start()

    blank = jnp.zeros((WM, WM), F32)

    def twice(part):
        return jnp.concatenate(
            [
                jnp.concatenate([part, blank], axis=1),
                jnp.concatenate([blank, part], axis=1),
            ],
            axis=0,
        )

    both_hi = jnp.transpose(twice(g_hi))
    both_lo = jnp.transpose(twice(g_lo))
    table = cast(
        jnp.concatenate(
            [
                jnp.concatenate([both_hi, both_lo], axis=1),
                jnp.concatenate([both_hi, jnp.zeros_like(both_lo)], axis=1),
            ],
            axis=0,
        )
    )
    row16 = iota((16, 256), 0)
    picks = (
        jnp.concatenate([top_hi, none, top_hi, none], axis=1),
        jnp.concatenate([none, top_hi, none, top_hi], axis=1),
        jnp.concatenate([top_lo, none, none, none], axis=1),
        jnp.concatenate([none, top_lo, none, none], axis=1),
    )
    query = jnp.zeros((16, 256), F32)
    for i, pick in enumerate(picks):
        query = jnp.where(row16 == i, pick, query)
    query = cast(query)

    def packed(x):
        hi, lo = split2(x)
        return cast(jnp.concatenate([hi, lo], axis=1))

    blocks = [slice(FB * b, FB * (b + 1)) for b in range(FACES // FB)]
    ys = [dot_nn(packed(force[cols, :]), table) for cols in blocks]
    for step in range(PICARD):
        rhs = []
        for cols, y in zip(blocks, ys):
            x = y[:, :128] + y[:, 128:]
            sq = x * x
            damping = 0.5 * lax.rsqrt(1.0 + sq + pltpu.roll(sq, WM, 1))
            rhs.append(packed(force[cols, :] - damping * x))
        if step < PICARD - 1:
            ys = [dot_nn(r, table) for r in rhs]
        else:
            ys = [dot_nt(query, r) for r in rhs]
    total = jnp.zeros((CS, 192), F32)
    for cols, y in zip(blocks, ys):
        nu = coef[1:2, cols]
        flux_u = nu * (y[0:1, :] + y[2:3, :])
        flux_w = nu * (y[1:2, :] + y[3:4, :])
        span_hot, pitch_hot = cell_tables(cell[:, cols])
        pieces = []
        for u_part, w_part in zip(split3(flux_u), split3(flux_w)):
            pieces.append(jnp.where(pitch_hot, u_part, 0.0))
            pieces.append(jnp.where(pitch_hot, w_part, 0.0))
        total = total + dot_nt(cast(span_hot), cast(jnp.concatenate(pieces, axis=0)))
    walls[...] = jnp.zeros((CS, 128), F32)
    walls[:, 0:64] = -0.5 * (total[:, 0:64] + total[:, 64:128] + total[:, 128:192])
    for copy in edges_out + give:
        copy.wait()


GROUP = 4
HALO = 8
ROWS = CS + 2 * HALO


def stencil_kernel(state, walls, prev_p, next_p, prev_s, next_s, out, kept, cur, work, sems):
    inner = pl.ds(HALO, CS)
    loads = []
    for c in range(4):
        for h in range(2):
            lanes = pl.ds(128 * h, 128)
            loads.append(
                pltpu.make_async_copy(
                    state.at[c, :, :, lanes], cur.at[h, c, pl.ds(1, CP), inner, :], sems.at[c]
                )
            )
            if c == 0:
                for plane, source in ((0, prev_p), (CP + 1, next_p)):
                    loads.append(
                        pltpu.make_async_copy(
                            source.at[:, :, lanes], cur.at[h, :, plane, inner, :], sems.at[4]
                        )
                    )
    for copy in loads:
        copy.start()

    flat = cur.reshape(2 * 4 * (CP + 2) * ROWS, 128)
    for h in range(2):
        lanes = slice(128 * h, 128 * h + 128)
        for c in range(4):
            for p in range(0, CP, 8):
                start = ((h * 4 + c) * (CP + 2) + 1 + p) * ROWS
                flat[pl.ds(start + HALO - 1, 8, stride=ROWS), :] = prev_s[c, p : p + 8, lanes]
                flat[pl.ds(start + HALO + CS, 8, stride=ROWS), :] = next_s[c, p : p + 8, lanes]

    i, j = iota((GN, GN), 0), iota((GN, GN), 1)
    near = jnp.where(jnp.abs(i - j) == 1, 1.0, 0.0)
    same = jnp.where((i == 0) | (i == GN - 1), 5.0, 4.0)
    matrix = jnp.where(i == j, same, near)
    matrix = cast(jnp.concatenate([matrix, matrix], axis=0))
    first_lane = iota((CS, 128), 1) == 0

    def put(c, h):
        lanes = pl.ds(128 * h, 128)
        return pltpu.make_async_copy(work.at[h, c], out.at[c, :, :, lanes], sems.at[5 + c])

    for copy in loads[0:6]:
        copy.wait()
    for c in range(4):
        if c > 0:
            loads[4 + 2 * c].wait()
            loads[5 + 2 * c].wait()

        def body(n, _):
            p = n * GROUP
            split = []
            for q in range(GROUP):
                a = cur[0, c, p + 1 + q, HALO : HALO + CS, :]
                b = cur[1, c, p + 1 + q, HALO : HALO + CS, :]
                a_hi, a_lo = split2(a)
                b_hi, b_lo = split2(b)
                split.append(jnp.concatenate([cast(x) for x in (a_hi, b_hi, a_lo, b_lo)], axis=1))
            y = dot_nn(jnp.concatenate(split, axis=0), matrix)
            for q in range(GROUP):
                for h in range(2):
                    up = cur[h, c, p + 1 + q, HALO + 1 : HALO + CS + 1, :]
                    dn = cur[h, c, p + 1 + q, HALO - 1 : HALO + CS - 1, :]
                    after = cur[h, c, p + 2 + q, HALO : HALO + CS, :]
                    prior = cur[h, c, p + q, HALO : HALO + CS, :]
                    mid = y[CS * q : CS * (q + 1), 128 * h : 128 * (h + 1)]
                    value = 0.1 * (mid + (up + dn)) + (0.25 * prior - 0.05 * after)
                    if c < 2 and h == 0:
                        wall = pltpu.roll(walls[...], 128 - (c * CP + p + q), 1)
                        value = value + jnp.where(first_lane, wall, 0.0)
                    if c == 2 and h == 0:
                        kept[p + q, :, :] = value
                    else:
                        work[h, c, p + q, :, :] = value
            return 0

        lax.fori_loop(0, CP // GROUP, body, 0)
        for h in range(2):
            if c != 2 or h == 1:
                put(c, h).start()
    for c in range(4):
        for h in range(2):
            if c != 2 or h == 1:
                put(c, h).wait()


def last_kernel(
    state, kept, recv, send, free, metal, owner, rank, top, coef, cell, wall_inv, metal_inv,
    out, metal_out,
    sems,
):
    corner_f = 0.5 * wall_inv[0:1, 0:1]
    corner_m = 0.5 * metal_inv[0:1, 0:1]
    got = recv[...]
    from_owner = jnp.transpose(got)[0:32, :]
    parts = cast(jnp.concatenate(split3(from_owner), axis=0))
    total = jnp.zeros((CS, 96), F32)
    for b in range(FACES // FB):
        cols = slice(FB * b, FB * (b + 1))
        hot = jnp.where(iota((DEV, FB), 0) == owner[:, cols], 1.0, 0.0)
        y = dot_nn(parts, cast(hot))
        y = y[0:32, :] + y[32:64, :] + y[64:96, :]
        which = iota((CAP, FB), 0) == rank[:, cols]
        v0 = jnp.sum(jnp.where(which, y[0:16, :], 0.0), axis=0, keepdims=True)
        km = jnp.sum(jnp.where(which, y[16:32, :], 0.0), axis=0, keepdims=True)
        kf = coef[0:1, cols]
        p = top[:, cols]
        tw = (kf * p + km * v0) / (kf * (1.0 - corner_f) + km * (1.0 - corner_m))
        heat = kf * (p + (corner_f - 1.0) * tw)
        span_hot, pitch_hot = cell_tables(cell[:, cols])
        pieces = [jnp.where(pitch_hot, part, 0.0) for part in split3(heat)]
        total = total + dot_nt(cast(span_hot), cast(jnp.concatenate(pieces, axis=0)))
    wall = -0.5 * (total[:, 0:32] + total[:, 32:64] + total[:, 64:96])
    wall = jnp.concatenate([wall, jnp.zeros((CS, 96), F32)], axis=1)
    first_lane = iota((CS, 128), 1) == 0
    for p in range(CP):
        column = wall if p == 0 else pltpu.roll(wall, 128 - p, 1)
        kept[p] = kept[p] + jnp.where(first_lane, column, 0.0)
    copy = pltpu.make_async_copy(kept, out.at[2, :, :, pl.ds(0, 128)], sems.at[0])
    copy.start()

    own = send[...]
    lane = iota((DEV, 128), 1)
    kf = pltpu.roll(got, 96, 1)
    p = pltpu.roll(got, 80, 1)
    km = pltpu.roll(own, 112, 1)
    valid = lane < CAP
    tw = (kf * p + km * own) / jnp.where(valid, kf * (1.0 - corner_f) + km * (1.0 - corner_m), 1.0)
    tw = jnp.where(valid, tw, 0.0)
    used = jnp.where(jnp.logical_and(valid, kf > 0.0), 1.0, 0.0)
    for step in (16, 32, 64):
        tw = tw + pltpu.roll(tw, step, 1)
        used = used + pltpu.roll(used, step, 1)
    mine = (lane >> 4) == (iota((DEV, 128), 0) & 7)
    tw = jnp.where(mine, tw, 0.0)
    used = jnp.where(mine, used, 0.0)
    gain = 0.5 * metal_inv[:, 0:1]
    for g in range(16):
        rows = slice(8 * g, 8 * g + 8)
        cols = slice(128 * g, 128 * g + 128)
        tw_row = jnp.sum(tw[rows, :], axis=0, keepdims=True)
        used_row = jnp.sum(used[rows, :], axis=0, keepdims=True)
        metal_out[:, cols] = jnp.where(
            used_row > 0.5, free[:, cols] + gain * tw_row, metal[:, cols]
        )
    copy.wait()


def spec(space):
    return pl.BlockSpec(memory_space=space)


ANY = pl.ANY
VM = pltpu.VMEM
HBM = pltpu.HBM


def shape(dims, dtype=F32):
    return jax.ShapeDtypeStruct(dims, dtype)


def params(limit=VMEM_LIMIT):
    return pltpu.CompilerParams(vmem_limit_bytes=limit)


def cost(microseconds):
    return pl.CostEstimate(
        flops=0, bytes_accessed=int(microseconds * 3_000_000), transcendentals=0
    )


def local(
    flow_state,
    wall_inverse,
    metal_inverse,
    metal_state,
    metal_conduct,
    face_coef,
    owner_map,
    face_cell,
    sample_col,
    sample_low,
):
    owner = owner_map.reshape(1, FACES)
    cell = face_cell.reshape(1, FACES)
    low = sample_low.reshape(1, FACES)
    conduct = metal_conduct.reshape(16, 128)
    send, first_p, last_p, first_s, last_s, rank, top, free, walls = pl.pallas_call(
        first_kernel,
        name="first",
        in_specs=[spec(HBM)] * 10,
        out_specs=[spec(ANY)] * 5 + [spec(VM)] * 4,
        out_shape=[
            shape((DEV, 128)),
            shape((4, CS, GN)),
            shape((4, CS, GN)),
            shape((4, CP, GN)),
            shape((4, CP, GN)),
            shape((1, FACES), I32),
            shape((1, FACES)),
            shape((MP, SLOT_DEV)),
            shape((CS, 128)),
        ],
        scratch_shapes=[
            pltpu.VMEM((8, COLS + PAD, 128), F32),
            pltpu.VMEM((FACES, 128), I32),
            pltpu.VMEM((FACES, 128), F32),
            pltpu.VMEM((FACES, 128), F32),
            pltpu.VMEM((DEV, 128), F32),
            pltpu.VMEM((2, 4, CS, GN), F32),
            pltpu.VMEM((2, 4, CP, GN), F32),
            pltpu.SemaphoreType.DMA((11,)),
            pltpu.SMEM((FACES,), I32),
            pltpu.VMEM((1, FACES), I32),
            pltpu.VMEM((1, FACES), I32),
            pltpu.VMEM((2, FACES), F32),
            pltpu.VMEM((1, FACES), I32),
            pltpu.VMEM((WM, WM), F32),
            pltpu.VMEM((MP, MP), F32),
            pltpu.VMEM((MP, SLOT_DEV), F32),
            pltpu.VMEM((16, 128), F32),
        ],
        compiler_params=params(VMEM_WHOLE),
        cost_estimate=cost(7),
    )(
        flow_state, sample_col, low, owner, face_coef, cell, wall_inverse, metal_inverse,
        metal_state, conduct,
    )

    recv = lax.all_to_all(send, AXES, split_axis=0, concat_axis=0, tiled=True)

    n_pitch, n_span = lax.axis_size("pitch"), lax.axis_size("span")
    up_p = [(i, (i + 1) % n_pitch) for i in range(n_pitch)]
    up_s = [(i, i + 1) for i in range(n_span - 1)]
    prev_p = lax.ppermute(last_p, "pitch", up_p)
    next_p = lax.ppermute(first_p, "pitch", [(j, i) for i, j in up_p])
    prev_s = lax.ppermute(last_s, "span", up_s)
    next_s = lax.ppermute(first_s, "span", [(j, i) for i, j in up_s])

    new_state, kept = pl.pallas_call(
        stencil_kernel,
        name="stencil",
        in_specs=[spec(ANY), spec(VM), spec(ANY), spec(ANY), spec(VM), spec(VM)],
        out_specs=[spec(ANY), spec(VM)],
        out_shape=[shape((4, CP, CS, GN)), shape((CP, CS, 128))],
        scratch_shapes=[
            pltpu.VMEM((2, 4, CP + 2, ROWS, 128), F32),
            pltpu.VMEM((2, 4, CP, CS, 128), F32),
            pltpu.SemaphoreType.DMA((9,)),
        ],
        compiler_params=params(),
        cost_estimate=cost(8),
    )(flow_state, walls, prev_p, next_p, prev_s, next_s)

    new_state, metal_out = pl.pallas_call(
        last_kernel,
        name="last",
        in_specs=[spec(ANY)] + [spec(VM)] * 12,
        out_specs=[spec(ANY), spec(VM)],
        out_shape=[shape((4, CP, CS, GN)), shape((MP, SLOT_DEV))],
        input_output_aliases={0: 0},
        scratch_shapes=[pltpu.SemaphoreType.DMA((1,))],
        compiler_params=params(),
        cost_estimate=cost(3),
    )(
        new_state, kept, recv, send, free, metal_state, owner, rank, top, face_coef, cell,
        wall_inverse, metal_inverse,
    )
    return (new_state, metal_out)


def solution(mesh):
    return jax.shard_map(
        local,
        mesh=mesh,
        in_specs=(
            P(None, "pitch", "span", None),
            P(),
            P(),
            P(None, ("pitch", "span")),
            P(("pitch", "span")),
            P(None, ("pitch", "span")),
            P(("pitch", "span"), None),
            P(("pitch", "span")),
            P(("pitch", "span")),
            P(("pitch", "span")),
        ),
        out_specs=(P(None, "pitch", "span", None), P(None, ("pitch", "span"))),
        check_vma=False,
    )
```

```python
import jax
import jax.numpy as jnp
from jax import lax
from jax.experimental import pallas as pl
from jax.experimental.pallas import tpu as pltpu
from jax.sharding import PartitionSpec as P

CP = 32
CS = 64
GN = 256
WM = 64
MP = 16
CAP = 16
DEV = 128
FACES = 1024
SLOT_DEV = 2048
COLS = CP * CS
PICARD = 3

F32 = jnp.float32
BF16 = jnp.bfloat16
I32 = jnp.int32
AXES = ("pitch", "span")
VMEM_LIMIT = 48 * 1024 * 1024
VMEM_WHOLE = 60 * 1024 * 1024
FB = 256
PAD = 8
ROOM = 32


def iota(shape, dim):
    return lax.broadcasted_iota(I32, shape, dim)


def dot_nn(a, b):
    return lax.dot_general(a, b, (((1,), (0,)), ((), ())), preferred_element_type=F32)


def dot_nt(a, b):
    return lax.dot_general(a, b, (((1,), (1,)), ((), ())), preferred_element_type=F32)


def split2(x):
    hi = x.astype(BF16).astype(F32)
    return hi, x - hi


def split3(x):
    hi = x.astype(BF16).astype(F32)
    rest = x - hi
    mid = rest.astype(BF16).astype(F32)
    return hi, mid, rest - mid


def cast(x):
    return x.astype(BF16)


def cell_tables(cell_row):
    width = cell_row.shape[1]
    span_hot = iota((CS, width), 0) == (cell_row & (CS - 1))
    pitch_hot = iota((CP, width), 0) == (cell_row >> 6)
    return jnp.where(span_hot, 1.0, 0.0), pitch_hot


def gather_lane(source, index):
    return jnp.take_along_axis(source, index, axis=1)


def pick_rows(refs, col_ref, base):
    sub = iota((8, 128), 0)
    blocks = [None] * len(refs)
    for i in range(8):
        at = col_ref[base + i]
        for k, ref in enumerate(refs):
            row = jnp.broadcast_to(ref[pl.ds(at, 1), :], (8, 128))
            blocks[k] = row if i == 0 else jnp.where(sub == i, row, blocks[k])
    return blocks


def first_kernel(
    state, *args,
):
    sources, (send, give_pa, give_pb, give_sa, give_sb, rank, top, free, force_out) = args[:9], args[9:18]
    cur, lowb, temp, force, out_send, edge_p, edge_s, sems, *held = args[18:]
    col, low, owner, coef, cell, wall_inv, metal_inv, metal, conduct = held
    small = [
        pltpu.make_async_copy(source, target, sems.at[9 + (i == 0)])
        for i, (source, target) in enumerate(zip(sources, held))
    ]
    for copy in small:
        copy.start()
    odd_p, odd_s = lax.axis_index("pitch") & 1, lax.axis_index("span") & 1
    columns = state.reshape(4, COLS, GN)
    loads = []
    for i, c in enumerate((2, 0, 1, 3)):
        for h in range(2):
            loads.append(
                pltpu.make_async_copy(
                    columns.at[c, :, pl.ds(128 * h, 128)],
                    cur.at[2 * c + h, pl.ds(0, COLS)],
                    sems.at[i],
                )
            )
    for copy in loads:
        copy.start()
    edges_in = [
        pltpu.make_async_copy(state.at[:, (1 - odd_p) * (CP - 1)], edge_p.at[0], sems.at[4]),
        pltpu.make_async_copy(state.at[:, odd_p * (CP - 1)], edge_p.at[1], sems.at[5]),
    ]
    for copy in edges_in:
        copy.start()

    for copy in small[1:]:
        copy.wait()

    eye = iota((128, 128), 0) == iota((128, 128), 1)
    ones = jnp.ones((128, 128), BF16)
    low_f = low[...].astype(F32)
    for b in range(FACES // 128):
        diag = jnp.where(eye, low_f[:, 128 * b : 128 * (b + 1)], 0.0)
        lowb[pl.ds(128 * b, 128), :] = dot_nn(cast(diag), ones).astype(I32)

    m = metal[...]
    inv = metal_inv[...]
    v = inv[:, 0:1] * m[0:1, :]
    for j in range(1, MP):
        v = v + inv[:, j : j + 1] * m[j : j + 1, :]
    free[...] = v
    v0 = jnp.concatenate([v[0:1, 128 * g : 128 * (g + 1)] for g in range(16)], axis=0)
    spread = jnp.where((iota((DEV, 16), 0) >> 3) == iota((DEV, 16), 1), 1.0, 0.0)
    parts = jnp.concatenate(split3(v0) + split3(conduct[...]), axis=1)
    wide = dot_nn(cast(spread), cast(parts))
    lane = iota((DEV, 128), 1)
    mine = (lane >> 4) == (iota((DEV, 128), 0) & 7)
    folded = []
    for k in range(2):
        a = wide[:, 384 * k : 384 * (k + 1)]
        y = jnp.where(mine, a[:, 0:128] + a[:, 128:256] + a[:, 256:384], 0.0)
        for step in (64, 32, 16):
            y = y + pltpu.roll(y, step, 1)
        folded.append(y)
    own_half = jnp.where(lane < 16, folded[0], folded[1])

    before = jnp.where(iota((FB, FB), 0) < iota((FB, FB), 1), 1.0, 0.0).astype(BF16)
    carry = jnp.zeros((DEV, 1), F32)
    for b in range(FACES // FB):
        cols = slice(FB * b, FB * (b + 1))
        hot = jnp.where(iota((DEV, FB), 0) == owner[:, cols], 1.0, 0.0)
        prior = dot_nn(cast(hot), before) + carry
        carry = carry + jnp.sum(hot, axis=1, keepdims=True)
        rank[:, cols] = jnp.sum(hot * prior, axis=0, keepdims=True).astype(I32)

    for copy in edges_in:
        copy.wait()
    edges_out = [
        pltpu.make_async_copy(edge_p.at[0], give_pa, sems.at[4]),
        pltpu.make_async_copy(edge_p.at[1], give_pb, sems.at[5]),
    ]
    for copy in edges_out:
        copy.start()
    small[0].wait()
    for copy in loads[0:6]:
        copy.wait()
    halves = [[cur.at[2 * c + h] for h in range(2)] for c in range(4)]
    lane8 = iota((8, 128), 1)
    left = lane8 < WM

    def body(g, _):
        base = g * 8
        index = lowb[pl.ds(base, 8), :] + (lane8 & (WM - 1))
        near = index < 128
        index = index & 127
        found = pick_rows([halves[c][h] for c in range(3) for h in range(2)], col, base)
        found = [gather_lane(x, index) for x in found]
        picked = [jnp.where(near, found[2 * c], found[2 * c + 1]) for c in range(3)]
        force[pl.ds(base, 8), :] = jnp.where(left, picked[0], picked[1])
        temp[pl.ds(base, 8), :] = picked[2]
        return 0

    lax.fori_loop(0, FACES // 8, body, 0, unroll=8)

    give = [pltpu.make_async_copy(force, force_out.at[0], sems.at[11])]
    give[0].start()

    g = wall_inv[...]
    g_hi, g_lo = split2(g)
    top_hi, top_lo = g_hi[0:1, :], g_lo[0:1, :]
    none = jnp.zeros((1, WM), F32)
    row16 = iota((16, 128), 0)
    query = jnp.where(
        row16 == 0,
        jnp.concatenate([top_hi, top_hi], axis=1),
        jnp.where(row16 == 1, jnp.concatenate([top_lo, none], axis=1), 0.0),
    )
    total = jnp.zeros((DEV, 128), F32)
    left_b = iota((FB, 128), 1) < WM
    for b in range(FACES // FB):
        cols = slice(FB * b, FB * (b + 1))
        x_hi, x_lo = split2(temp[cols, :])
        p = dot_nt(cast(query), cast(jnp.where(left_b, x_hi, x_lo)))
        p = p[0:1, :] + p[1:2, :]
        top[:, cols] = p
        hot = jnp.where(iota((DEV, FB), 0) == owner[:, cols], 1.0, 0.0)
        which = iota((CAP, FB), 0) == rank[:, cols]
        kf_parts = split3(coef[0:1, cols])
        p_parts = split3(p)
        pieces = [jnp.zeros((32, FB), F32)]
        for kf_part, p_part in zip(kf_parts, p_parts):
            pieces.append(jnp.where(which, kf_part, 0.0))
            pieces.append(jnp.where(which, p_part, 0.0))
        total = total + dot_nt(cast(hot), cast(jnp.concatenate(pieces, axis=0)))
    total = total + pltpu.roll(total, 96, 1) + pltpu.roll(total, 64, 1)
    out_send[...] = jnp.where(lane < 32, own_half, jnp.where(lane < 64, total, 0.0))
    give.append(pltpu.make_async_copy(out_send, send, sems.at[6]))
    give[1].start()

    for copy in loads[6:]:
        copy.wait()
    for c in range(4):
        for h in range(2):
            lanes = slice(128 * h, 128 * h + 128)
            for p in range(0, CP, 8):
                for k, row in enumerate(((1 - odd_s) * (CS - 1), odd_s * (CS - 1))):
                    edge_s[k, c, p : p + 8, lanes] = halves[c][h][
                        pl.ds(p * CS + row, 8, stride=CS), :
                    ]
    give.append(pltpu.make_async_copy(edge_s.at[0], give_sa, sems.at[7]))
    give.append(pltpu.make_async_copy(edge_s.at[1], give_sb, sems.at[8]))
    give[-1].start()
    give[-2].start()
    for copy in edges_out + give:
        copy.wait()


def drag(force, coef, cell, wall_inv, walls):
    g_hi, g_lo = split2(wall_inv[...])
    top_hi, top_lo = g_hi[0:1, :], g_lo[0:1, :]
    none = jnp.zeros((1, WM), F32)
    blank = jnp.zeros((WM, WM), F32)

    def twice(part):
        return jnp.concatenate(
            [
                jnp.concatenate([part, blank], axis=1),
                jnp.concatenate([blank, part], axis=1),
            ],
            axis=0,
        )

    both_hi = jnp.transpose(twice(g_hi))
    both_lo = jnp.transpose(twice(g_lo))
    table = cast(
        jnp.concatenate(
            [
                jnp.concatenate([both_hi, both_lo], axis=1),
                jnp.concatenate([both_hi, jnp.zeros_like(both_lo)], axis=1),
            ],
            axis=0,
        )
    )
    row16 = iota((16, 256), 0)
    picks = (
        jnp.concatenate([top_hi, none, top_hi, none], axis=1),
        jnp.concatenate([none, top_hi, none, top_hi], axis=1),
        jnp.concatenate([top_lo, none, none, none], axis=1),
        jnp.concatenate([none, top_lo, none, none], axis=1),
    )
    query = jnp.zeros((16, 256), F32)
    for i, pick in enumerate(picks):
        query = jnp.where(row16 == i, pick, query)
    query = cast(query)

    def packed(x):
        hi, lo = split2(x)
        return cast(jnp.concatenate([hi, lo], axis=1))

    blocks = [slice(FB * b, FB * (b + 1)) for b in range(FACES // FB)]
    ys = [dot_nn(packed(force[cols, :]), table) for cols in blocks]
    for step in range(PICARD):
        rhs = []
        for cols, y in zip(blocks, ys):
            x = y[:, :128] + y[:, 128:]
            sq = x * x
            damping = 0.5 * lax.rsqrt(1.0 + sq + pltpu.roll(sq, WM, 1))
            rhs.append(packed(force[cols, :] - damping * x))
        if step < PICARD - 1:
            ys = [dot_nn(r, table) for r in rhs]
        else:
            ys = [dot_nt(query, r) for r in rhs]
    total = jnp.zeros((CS, 192), F32)
    for cols, y in zip(blocks, ys):
        nu = coef[1:2, cols]
        flux_u = nu * (y[0:1, :] + y[2:3, :])
        flux_w = nu * (y[1:2, :] + y[3:4, :])
        span_hot, pitch_hot = cell_tables(cell[:, cols])
        pieces = []
        for u_part, w_part in zip(split3(flux_u), split3(flux_w)):
            pieces.append(jnp.where(pitch_hot, u_part, 0.0))
            pieces.append(jnp.where(pitch_hot, w_part, 0.0))
        total = total + dot_nt(cast(span_hot), cast(jnp.concatenate(pieces, axis=0)))
    walls[...] = jnp.zeros((CS, 128), F32)
    walls[:, 0:64] = -0.5 * (total[:, 0:64] + total[:, 64:128] + total[:, 128:192])


GROUP = 4
HALO = 8
ROWS = CS + 2 * HALO


def stencil_kernel(
    state, force_in, coef, cell, wall_inv, got_pa, got_pb, got_sa, got_sb,
    out, kept,
    cur, work, force, walls, y_even, y_odd, sems,
):
    odd_p, odd_s = lax.axis_index("pitch") & 1, lax.axis_index("span") & 1
    inner = pl.ds(HALO, CS)
    bring = pltpu.make_async_copy(force_in.at[0], force, sems.at[9])
    bring.start()
    loads = []
    for c in range(4):
        for h in range(2):
            lanes = pl.ds(128 * h, 128)
            loads.append(
                pltpu.make_async_copy(
                    state.at[c, :, :, lanes], cur.at[h, c, pl.ds(1, CP), inner, :], sems.at[c]
                )
            )
    edges = []
    for h in range(2):
        lanes = pl.ds(128 * h, 128)
        for plane, source in (((1 - odd_p) * (CP + 1), got_pa), (odd_p * (CP + 1), got_pb)):
            edges.append(
                pltpu.make_async_copy(
                    source.at[:, :, lanes], cur.at[h, :, plane, inner, :], sems.at[4]
                )
            )
    for copy in loads[:2] + edges + loads[2:]:
        copy.start()

    flat = cur.reshape(2 * 4 * (CP + 2) * ROWS, 128)
    below, above = HALO - 1, HALO + CS
    row_a = above + odd_s * (below - above)
    row_b = below + odd_s * (above - below)
    for h in range(2):
        lanes = slice(128 * h, 128 * h + 128)
        for c in range(4):
            for p in range(0, CP, 8):
                start = ((h * 4 + c) * (CP + 2) + 1 + p) * ROWS
                flat[pl.ds(start + row_a, 8, stride=ROWS), :] = got_sa[c, p : p + 8, lanes]
                flat[pl.ds(start + row_b, 8, stride=ROWS), :] = got_sb[c, p : p + 8, lanes]

    bring.wait()
    drag(force, coef, cell, wall_inv, walls)

    i, j = iota((GN, GN), 0), iota((GN, GN), 1)
    near = jnp.where(jnp.abs(i - j) == 1, 1.0, 0.0)
    same = jnp.where((i == 0) | (i == GN - 1), 5.0, 4.0)
    matrix = jnp.where(i == j, same, near)
    matrix = cast(jnp.concatenate([matrix, matrix], axis=0))
    first_lane = iota((CS, 128), 1) == 0

    def put(c, h):
        lanes = pl.ds(128 * h, 128)
        return pltpu.make_async_copy(work.at[h, c], out.at[c, :, :, lanes], sems.at[5 + c])

    steps = CP // GROUP

    def along(t, y):
        c, p = t // steps, (t % steps) * GROUP
        split = []
        for q in range(GROUP):
            a_hi, a_lo = split2(cur[0, c, p + 1 + q, HALO : HALO + CS, :])
            b_hi, b_lo = split2(cur[1, c, p + 1 + q, HALO : HALO + CS, :])
            split.append(jnp.concatenate([cast(x) for x in (a_hi, b_hi, a_lo, b_lo)], axis=1))
        y[...] = dot_nn(jnp.concatenate(split, axis=0), matrix)

    def finish(c, n, y):
        p = n * GROUP
        for q in range(GROUP):
            for h in range(2):
                up = cur[h, c, p + 1 + q, HALO + 1 : HALO + CS + 1, :]
                dn = cur[h, c, p + 1 + q, HALO - 1 : HALO + CS - 1, :]
                after = cur[h, c, p + 2 + q, HALO : HALO + CS, :]
                prior = cur[h, c, p + q, HALO : HALO + CS, :]
                mid = y[CS * q : CS * (q + 1), 128 * h : 128 * (h + 1)]
                value = 0.1 * (mid + (up + dn)) + (0.25 * prior - 0.05 * after)
                if c < 2 and h == 0:
                    wall = pltpu.roll(walls[...], 128 - (c * CP + p + q), 1)
                    value = value + jnp.where(first_lane, wall, 0.0)
                if c == 2 and h == 0:
                    kept[p + q, :, :] = value
                else:
                    work[h, c, p + q, :, :] = value

    for copy in loads[:2] + edges:
        copy.wait()
    along(0, y_even)
    for c in range(4):
        if c < 3:
            for copy in loads[2 * c + 2 : 2 * c + 4]:
                copy.wait()

        def body(n, _):
            t = c * steps + 2 * n
            along(t + 1, y_odd)
            finish(c, 2 * n, y_even)
            along(jnp.minimum(t + 2, 4 * steps - 1), y_even)
            finish(c, 2 * n + 1, y_odd)
            return 0

        lax.fori_loop(0, steps // 2, body, 0)
        for h in range(2):
            if c != 2 or h == 1:
                put(c, h).start()
    for c in range(4):
        for h in range(2):
            if c != 2 or h == 1:
                put(c, h).wait()


def last_kernel(
    state, kept, recv, send, free, metal, owner, rank, top, coef, cell, wall_inv, metal_inv,
    out, metal_give,
    metal_out, sems,
):
    corner_f = 0.5 * wall_inv[0:1, 0:1]
    corner_m = 0.5 * metal_inv[0:1, 0:1]
    got = recv[...]
    from_owner = jnp.transpose(got)[0:32, :]
    parts = cast(jnp.concatenate(split3(from_owner), axis=0))
    total = jnp.zeros((CS, 96), F32)
    for b in range(FACES // FB):
        cols = slice(FB * b, FB * (b + 1))
        hot = jnp.where(iota((DEV, FB), 0) == owner[:, cols], 1.0, 0.0)
        y = dot_nn(parts, cast(hot))
        y = y[0:32, :] + y[32:64, :] + y[64:96, :]
        which = iota((CAP, FB), 0) == rank[:, cols]
        v0 = jnp.sum(jnp.where(which, y[0:16, :], 0.0), axis=0, keepdims=True)
        km = jnp.sum(jnp.where(which, y[16:32, :], 0.0), axis=0, keepdims=True)
        kf = coef[0:1, cols]
        p = top[:, cols]
        tw = (kf * p + km * v0) / (kf * (1.0 - corner_f) + km * (1.0 - corner_m))
        heat = kf * (p + (corner_f - 1.0) * tw)
        span_hot, pitch_hot = cell_tables(cell[:, cols])
        pieces = [jnp.where(pitch_hot, part, 0.0) for part in split3(heat)]
        total = total + dot_nt(cast(span_hot), cast(jnp.concatenate(pieces, axis=0)))
    wall = -0.5 * (total[:, 0:32] + total[:, 32:64] + total[:, 64:96])
    wall = jnp.concatenate([wall, jnp.zeros((CS, 96), F32)], axis=1)
    first_lane = iota((CS, 128), 1) == 0
    for p in range(CP):
        column = wall if p == 0 else pltpu.roll(wall, 128 - p, 1)
        kept[p] = kept[p] + jnp.where(first_lane, column, 0.0)
    copy = pltpu.make_async_copy(kept, out.at[2, :, :, pl.ds(0, 128)], sems.at[0])
    copy.start()

    own = send[...]
    lane = iota((DEV, 128), 1)
    kf = pltpu.roll(got, 96, 1)
    p = pltpu.roll(got, 80, 1)
    km = pltpu.roll(own, 112, 1)
    valid = lane < CAP
    tw = (kf * p + km * own) / jnp.where(valid, kf * (1.0 - corner_f) + km * (1.0 - corner_m), 1.0)
    tw = jnp.where(valid, tw, 0.0)
    used = jnp.where(jnp.logical_and(valid, kf > 0.0), 1.0, 0.0)
    for step in (16, 32, 64):
        tw = tw + pltpu.roll(tw, step, 1)
        used = used + pltpu.roll(used, step, 1)
    mine = (lane >> 4) == (iota((DEV, 128), 0) & 7)
    tw = jnp.where(mine, tw, 0.0)
    used = jnp.where(mine, used, 0.0)
    gain = 0.5 * metal_inv[:, 0:1]
    for g in range(16):
        rows = slice(8 * g, 8 * g + 8)
        cols = slice(128 * g, 128 * g + 128)
        tw_row = jnp.sum(tw[rows, :], axis=0, keepdims=True)
        used_row = jnp.sum(used[rows, :], axis=0, keepdims=True)
        metal_out[:, cols] = jnp.where(
            used_row > 0.5, free[:, cols] + gain * tw_row, metal[:, cols]
        )
    give = pltpu.make_async_copy(metal_out, metal_give, sems.at[1])
    give.start()
    give.wait()
    copy.wait()


def spec(space):
    return pl.BlockSpec(memory_space=space)


ANY = pl.ANY
VM = pltpu.VMEM
HBM = pltpu.HBM


def shape(dims, dtype=F32):
    return jax.ShapeDtypeStruct(dims, dtype)


def params(limit=VMEM_LIMIT):
    return pltpu.CompilerParams(vmem_limit_bytes=limit)


def cost(microseconds):
    return pl.CostEstimate(
        flops=0, bytes_accessed=int(microseconds * 3_000_000), transcendentals=0
    )


def local(
    flow_state,
    wall_inverse,
    metal_inverse,
    metal_state,
    metal_conduct,
    face_coef,
    owner_map,
    face_cell,
    sample_col,
    sample_low,
):
    owner = owner_map.reshape(1, FACES)
    cell = face_cell.reshape(1, FACES)
    low = sample_low.reshape(1, FACES)
    conduct = metal_conduct.reshape(16, 128)
    send, give_pa, give_pb, give_sa, give_sb, rank, top, free, force = pl.pallas_call(
        first_kernel,
        name="first",
        in_specs=[spec(HBM)] * 10,
        out_specs=[spec(HBM)] * 5 + [spec(VM)] * 3 + [spec(HBM)],
        out_shape=[
            shape((DEV, 128)),
            shape((4, CS, GN)),
            shape((4, CS, GN)),
            shape((4, CP, GN)),
            shape((4, CP, GN)),
            shape((1, FACES), I32),
            shape((1, FACES)),
            shape((MP, SLOT_DEV)),
            shape((ROOM, FACES, 128)),
        ],
        scratch_shapes=[
            pltpu.VMEM((8, COLS + PAD, 128), F32),
            pltpu.VMEM((FACES, 128), I32),
            pltpu.VMEM((FACES, 128), F32),
            pltpu.VMEM((FACES, 128), F32),
            pltpu.VMEM((DEV, 128), F32),
            pltpu.VMEM((2, 4, CS, GN), F32),
            pltpu.VMEM((2, 4, CP, GN), F32),
            pltpu.SemaphoreType.DMA((12,)),
            pltpu.SMEM((FACES,), I32),
            pltpu.VMEM((1, FACES), I32),
            pltpu.VMEM((1, FACES), I32),
            pltpu.VMEM((2, FACES), F32),
            pltpu.VMEM((1, FACES), I32),
            pltpu.VMEM((WM, WM), F32),
            pltpu.VMEM((MP, MP), F32),
            pltpu.VMEM((MP, SLOT_DEV), F32),
            pltpu.VMEM((16, 128), F32),
        ],
        compiler_params=params(VMEM_WHOLE),
        cost_estimate=cost(7),
    )(
        flow_state, sample_col, low, owner, face_coef, cell, wall_inverse, metal_inverse,
        metal_state, conduct,
    )

    recv = lax.all_to_all(send, AXES, split_axis=0, concat_axis=0, tiled=True)

    n_pitch, n_span = lax.axis_size("pitch"), lax.axis_size("span")
    within_p = [(i, i ^ 1) for i in range(n_pitch)]
    across_p = [(i, (i + (1 if i & 1 else -1)) % n_pitch) for i in range(n_pitch)]
    within_s = [(i, i ^ 1) for i in range(n_span)]
    across_s = [(i, i + (1 if i & 1 else -1)) for i in range(1, n_span - 1)]
    got_pa = lax.ppermute(give_pa, "pitch", within_p)
    got_pb = lax.ppermute(give_pb, "pitch", across_p)
    got_sa = lax.ppermute(give_sa, "span", within_s)
    got_sb = lax.ppermute(give_sb, "span", across_s)

    new_state, kept = pl.pallas_call(
        stencil_kernel,
        name="stencil",
        in_specs=[spec(ANY), spec(ANY)] + [spec(VM)] * 3 + [spec(ANY)] * 2 + [spec(VM)] * 2,
        out_specs=[spec(ANY), spec(VM)],
        out_shape=[shape((4, CP, CS, GN)), shape((CP, CS, 128))],
        scratch_shapes=[
            pltpu.VMEM((2, 4, CP + 2, ROWS, 128), F32),
            pltpu.VMEM((2, 4, CP, CS, 128), F32),
            pltpu.VMEM((FACES, 128), F32),
            pltpu.VMEM((CS, 128), F32),
            pltpu.VMEM((GROUP * CS, GN), F32),
            pltpu.VMEM((GROUP * CS, GN), F32),
            pltpu.SemaphoreType.DMA((10,)),
        ],
        compiler_params=params(),
        cost_estimate=cost(10),
    )(flow_state, force, face_coef, cell, wall_inverse, got_pa, got_pb, got_sa, got_sb)

    new_state, metal_out = pl.pallas_call(
        last_kernel,
        name="last",
        in_specs=[spec(ANY)] + [spec(VM)] * 12,
        out_specs=[spec(ANY), spec(HBM)],
        out_shape=[shape((4, CP, CS, GN)), shape((MP, SLOT_DEV))],
        input_output_aliases={0: 0},
        scratch_shapes=[pltpu.VMEM((MP, SLOT_DEV), F32), pltpu.SemaphoreType.DMA((2,))],
        compiler_params=params(),
        cost_estimate=cost(3),
    )(
        new_state, kept, recv, send, free, metal_state, owner, rank, top, face_coef, cell,
        wall_inverse, metal_inverse,
    )
    return (new_state, metal_out)


def solution(mesh):
    return jax.shard_map(
        local,
        mesh=mesh,
        in_specs=(
            P(None, "pitch", "span", None),
            P(),
            P(),
            P(None, ("pitch", "span")),
            P(("pitch", "span")),
            P(None, ("pitch", "span")),
            P(("pitch", "span"), None),
            P(("pitch", "span")),
            P(("pitch", "span")),
            P(("pitch", "span")),
        ),
        out_specs=(P(None, "pitch", "span", None), P(None, ("pitch", "span"))),
        check_vma=False,
    )
```

```python
import jax
import jax.numpy as jnp
from jax import lax
from jax.experimental import pallas as pl
from jax.experimental.pallas import tpu as pltpu
from jax.sharding import PartitionSpec as P

CP = 32
CS = 64
GN = 256
WM = 64
MP = 16
CAP = 16
DEV = 128
FACES = 1024
SLOT_DEV = 2048
COLS = CP * CS
PICARD = 3

F32 = jnp.float32
BF16 = jnp.bfloat16
I32 = jnp.int32
AXES = ("pitch", "span")
VMEM_LIMIT = 48 * 1024 * 1024
VMEM_WHOLE = 60 * 1024 * 1024
FB = 256
PAD = 8
ROOM = 32


def iota(shape, dim):
    return lax.broadcasted_iota(I32, shape, dim)


def dot_nn(a, b):
    return lax.dot_general(a, b, (((1,), (0,)), ((), ())), preferred_element_type=F32)


def dot_nt(a, b):
    return lax.dot_general(a, b, (((1,), (1,)), ((), ())), preferred_element_type=F32)


def split2(x):
    hi = x.astype(BF16).astype(F32)
    return hi, x - hi


def split3(x):
    hi = x.astype(BF16).astype(F32)
    rest = x - hi
    mid = rest.astype(BF16).astype(F32)
    return hi, mid, rest - mid


def cast(x):
    return x.astype(BF16)


def cell_tables(cell_row):
    width = cell_row.shape[1]
    span_hot = iota((CS, width), 0) == (cell_row & (CS - 1))
    pitch_hot = iota((CP, width), 0) == (cell_row >> 6)
    return jnp.where(span_hot, 1.0, 0.0), pitch_hot


def gather_lane(source, index):
    return jnp.take_along_axis(source, index, axis=1)


def pick_rows(refs, col_ref, base):
    sub = iota((8, 128), 0)
    blocks = [None] * len(refs)
    for i in range(8):
        at = col_ref[base + i]
        for k, ref in enumerate(refs):
            row = jnp.broadcast_to(ref[pl.ds(at, 1), :], (8, 128))
            blocks[k] = row if i == 0 else jnp.where(sub == i, row, blocks[k])
    return blocks


def first_kernel(
    state, *args,
):
    sources, (send, give_pa, give_pb, give_sa, give_sb, rank, top, free, force_out) = args[:9], args[9:18]
    cur, lowb, temp, force, out_send, edge_p, edge_s, sems, *held = args[18:]
    col, low, owner, coef, cell, wall_inv, metal_inv, metal, conduct = held
    small = [
        pltpu.make_async_copy(source, target, sems.at[9 + (i == 0)])
        for i, (source, target) in enumerate(zip(sources, held))
    ]
    for copy in small:
        copy.start()
    odd_p, odd_s = lax.axis_index("pitch") & 1, lax.axis_index("span") & 1
    columns = state.reshape(4, COLS, GN)
    loads = []
    for i, c in enumerate((2, 0, 1, 3)):
        for h in range(2):
            loads.append(
                pltpu.make_async_copy(
                    columns.at[c, :, pl.ds(128 * h, 128)],
                    cur.at[2 * c + h, pl.ds(0, COLS)],
                    sems.at[i],
                )
            )
    for copy in loads[:6]:
        copy.start()
    edges_in = [
        pltpu.make_async_copy(state.at[:, (1 - odd_p) * (CP - 1)], edge_p.at[0], sems.at[4]),
        pltpu.make_async_copy(state.at[:, odd_p * (CP - 1)], edge_p.at[1], sems.at[5]),
    ]

    for copy in small[1:]:
        copy.wait()

    eye = iota((128, 128), 0) == iota((128, 128), 1)
    ones = jnp.ones((128, 128), BF16)
    low_f = low[...].astype(F32)
    for b in range(FACES // 128):
        diag = jnp.where(eye, low_f[:, 128 * b : 128 * (b + 1)], 0.0)
        lowb[pl.ds(128 * b, 128), :] = dot_nn(cast(diag), ones).astype(I32)

    m = metal[...]
    inv = metal_inv[...]
    v = inv[:, 0:1] * m[0:1, :]
    for j in range(1, MP):
        v = v + inv[:, j : j + 1] * m[j : j + 1, :]
    free[...] = v
    v0 = jnp.concatenate([v[0:1, 128 * g : 128 * (g + 1)] for g in range(16)], axis=0)
    spread = jnp.where((iota((DEV, 16), 0) >> 3) == iota((DEV, 16), 1), 1.0, 0.0)
    parts = jnp.concatenate(split3(v0) + split3(conduct[...]), axis=1)
    wide = dot_nn(cast(spread), cast(parts))
    lane = iota((DEV, 128), 1)
    mine = (lane >> 4) == (iota((DEV, 128), 0) & 7)
    folded = []
    for k in range(2):
        a = wide[:, 384 * k : 384 * (k + 1)]
        y = jnp.where(mine, a[:, 0:128] + a[:, 128:256] + a[:, 256:384], 0.0)
        for step in (64, 32, 16):
            y = y + pltpu.roll(y, step, 1)
        folded.append(y)
    own_half = jnp.where(lane < 16, folded[0], folded[1])

    before = jnp.where(iota((FB, FB), 0) < iota((FB, FB), 1), 1.0, 0.0).astype(BF16)
    carry = jnp.zeros((DEV, 1), F32)
    for b in range(FACES // FB):
        cols = slice(FB * b, FB * (b + 1))
        hot = jnp.where(iota((DEV, FB), 0) == owner[:, cols], 1.0, 0.0)
        prior = dot_nn(cast(hot), before) + carry
        carry = carry + jnp.sum(hot, axis=1, keepdims=True)
        rank[:, cols] = jnp.sum(hot * prior, axis=0, keepdims=True).astype(I32)

    small[0].wait()
    for copy in loads[:6]:
        copy.wait()
    for copy in loads[6:] + edges_in:
        copy.start()
    halves = [[cur.at[2 * c + h] for h in range(2)] for c in range(4)]
    lane8 = iota((8, 128), 1)
    left = lane8 < WM

    def body(g, _):
        base = g * 8
        index = lowb[pl.ds(base, 8), :] + (lane8 & (WM - 1))
        near = index < 128
        index = index & 127
        found = pick_rows([halves[c][h] for c in range(3) for h in range(2)], col, base)
        found = [gather_lane(x, index) for x in found]
        picked = [jnp.where(near, found[2 * c], found[2 * c + 1]) for c in range(3)]
        force[pl.ds(base, 8), :] = jnp.where(left, picked[0], picked[1])
        temp[pl.ds(base, 8), :] = picked[2]
        return 0

    lax.fori_loop(0, FACES // 8, body, 0, unroll=8)

    give = [pltpu.make_async_copy(force, force_out.at[0], sems.at[11])]
    give[0].start()

    g = wall_inv[...]
    g_hi, g_lo = split2(g)
    top_hi, top_lo = g_hi[0:1, :], g_lo[0:1, :]
    none = jnp.zeros((1, WM), F32)
    row16 = iota((16, 128), 0)
    query = jnp.where(
        row16 == 0,
        jnp.concatenate([top_hi, top_hi], axis=1),
        jnp.where(row16 == 1, jnp.concatenate([top_lo, none], axis=1), 0.0),
    )
    total = jnp.zeros((DEV, 128), F32)
    left_b = iota((FB, 128), 1) < WM
    for b in range(FACES // FB):
        cols = slice(FB * b, FB * (b + 1))
        x_hi, x_lo = split2(temp[cols, :])
        p = dot_nt(cast(query), cast(jnp.where(left_b, x_hi, x_lo)))
        p = p[0:1, :] + p[1:2, :]
        top[:, cols] = p
        hot = jnp.where(iota((DEV, FB), 0) == owner[:, cols], 1.0, 0.0)
        which = iota((CAP, FB), 0) == rank[:, cols]
        kf_parts = split3(coef[0:1, cols])
        p_parts = split3(p)
        pieces = [jnp.zeros((32, FB), F32)]
        for kf_part, p_part in zip(kf_parts, p_parts):
            pieces.append(jnp.where(which, kf_part, 0.0))
            pieces.append(jnp.where(which, p_part, 0.0))
        total = total + dot_nt(cast(hot), cast(jnp.concatenate(pieces, axis=0)))
    total = total + pltpu.roll(total, 96, 1) + pltpu.roll(total, 64, 1)
    out_send[...] = jnp.where(lane < 32, own_half, jnp.where(lane < 64, total, 0.0))
    give.append(pltpu.make_async_copy(out_send, send, sems.at[6]))
    give[1].start()

    for copy in loads[6:] + edges_in:
        copy.wait()
    edges_out = [
        pltpu.make_async_copy(edge_p.at[0], give_pa, sems.at[4]),
        pltpu.make_async_copy(edge_p.at[1], give_pb, sems.at[5]),
    ]
    for copy in edges_out:
        copy.start()
    for c in range(4):
        for h in range(2):
            lanes = slice(128 * h, 128 * h + 128)
            for p in range(0, CP, 8):
                for k, row in enumerate(((1 - odd_s) * (CS - 1), odd_s * (CS - 1))):
                    edge_s[k, c, p : p + 8, lanes] = halves[c][h][
                        pl.ds(p * CS + row, 8, stride=CS), :
                    ]
    give.append(pltpu.make_async_copy(edge_s.at[0], give_sa, sems.at[7]))
    give.append(pltpu.make_async_copy(edge_s.at[1], give_sb, sems.at[8]))
    give[-1].start()
    give[-2].start()
    for copy in edges_out + give:
        copy.wait()


def drag(force, coef, cell, wall_inv, walls):
    g_hi, g_lo = split2(wall_inv[...])
    top_hi, top_lo = g_hi[0:1, :], g_lo[0:1, :]
    none = jnp.zeros((1, WM), F32)
    blank = jnp.zeros((WM, WM), F32)

    def twice(part):
        return jnp.concatenate(
            [
                jnp.concatenate([part, blank], axis=1),
                jnp.concatenate([blank, part], axis=1),
            ],
            axis=0,
        )

    both_hi = jnp.transpose(twice(g_hi))
    both_lo = jnp.transpose(twice(g_lo))
    table = cast(
        jnp.concatenate(
            [
                jnp.concatenate([both_hi, both_lo], axis=1),
                jnp.concatenate([both_hi, jnp.zeros_like(both_lo)], axis=1),
            ],
            axis=0,
        )
    )
    row16 = iota((16, 256), 0)
    picks = (
        jnp.concatenate([top_hi, none, top_hi, none], axis=1),
        jnp.concatenate([none, top_hi, none, top_hi], axis=1),
        jnp.concatenate([top_lo, none, none, none], axis=1),
        jnp.concatenate([none, top_lo, none, none], axis=1),
    )
    query = jnp.zeros((16, 256), F32)
    for i, pick in enumerate(picks):
        query = jnp.where(row16 == i, pick, query)
    query = cast(query)

    def packed(x):
        hi, lo = split2(x)
        return cast(jnp.concatenate([hi, lo], axis=1))

    blocks = [slice(FB * b, FB * (b + 1)) for b in range(FACES // FB)]
    ys = [dot_nn(packed(force[cols, :]), table) for cols in blocks]
    for step in range(PICARD):
        rhs = []
        for cols, y in zip(blocks, ys):
            x = y[:, :128] + y[:, 128:]
            sq = x * x
            damping = 0.5 * lax.rsqrt(1.0 + sq + pltpu.roll(sq, WM, 1))
            rhs.append(packed(force[cols, :] - damping * x))
        if step < PICARD - 1:
            ys = [dot_nn(r, table) for r in rhs]
        else:
            ys = [dot_nt(query, r) for r in rhs]
    total = jnp.zeros((CS, 192), F32)
    for cols, y in zip(blocks, ys):
        nu = coef[1:2, cols]
        flux_u = nu * (y[0:1, :] + y[2:3, :])
        flux_w = nu * (y[1:2, :] + y[3:4, :])
        span_hot, pitch_hot = cell_tables(cell[:, cols])
        pieces = []
        for u_part, w_part in zip(split3(flux_u), split3(flux_w)):
            pieces.append(jnp.where(pitch_hot, u_part, 0.0))
            pieces.append(jnp.where(pitch_hot, w_part, 0.0))
        total = total + dot_nt(cast(span_hot), cast(jnp.concatenate(pieces, axis=0)))
    walls[...] = jnp.zeros((CS, 128), F32)
    walls[:, 0:64] = -0.5 * (total[:, 0:64] + total[:, 64:128] + total[:, 128:192])


GROUP = 4
HALO = 8
ROWS = CS + 2 * HALO


def stencil_kernel(
    state, force_in, coef, cell, wall_inv, got_pa, got_pb, got_sa, got_sb,
    out, kept,
    cur, work, force, walls, y_even, y_odd, sems,
):
    odd_p, odd_s = lax.axis_index("pitch") & 1, lax.axis_index("span") & 1
    inner = pl.ds(HALO, CS)
    bring = pltpu.make_async_copy(force_in.at[0], force, sems.at[9])
    bring.start()
    loads = []
    for c in range(4):
        for h in range(2):
            lanes = pl.ds(128 * h, 128)
            loads.append(
                pltpu.make_async_copy(
                    state.at[c, :, :, lanes], cur.at[h, c, pl.ds(1, CP), inner, :], sems.at[c]
                )
            )
    edges = []
    for h in range(2):
        lanes = pl.ds(128 * h, 128)
        for plane, source in (((1 - odd_p) * (CP + 1), got_pa), (odd_p * (CP + 1), got_pb)):
            edges.append(
                pltpu.make_async_copy(
                    source.at[:, :, lanes], cur.at[h, :, plane, inner, :], sems.at[4]
                )
            )
    for copy in loads[:2] + edges + loads[2:]:
        copy.start()

    flat = cur.reshape(2 * 4 * (CP + 2) * ROWS, 128)
    below, above = HALO - 1, HALO + CS
    row_a = above + odd_s * (below - above)
    row_b = below + odd_s * (above - below)
    for h in range(2):
        lanes = slice(128 * h, 128 * h + 128)
        for c in range(4):
            for p in range(0, CP, 8):
                start = ((h * 4 + c) * (CP + 2) + 1 + p) * ROWS
                flat[pl.ds(start + row_a, 8, stride=ROWS), :] = got_sa[c, p : p + 8, lanes]
                flat[pl.ds(start + row_b, 8, stride=ROWS), :] = got_sb[c, p : p + 8, lanes]

    bring.wait()
    drag(force, coef, cell, wall_inv, walls)

    i, j = iota((GN, GN), 0), iota((GN, GN), 1)
    near = jnp.where(jnp.abs(i - j) == 1, 1.0, 0.0)
    same = jnp.where((i == 0) | (i == GN - 1), 5.0, 4.0)
    matrix = cast(jnp.where(i == j, same, near))
    first_lane = iota((CS, 128), 1) == 0

    def put(c, h, planes):
        lanes = pl.ds(128 * h, 128)
        return pltpu.make_async_copy(
            work.at[h, c, planes], out.at[c, planes, :, lanes], sems.at[5 + c]
        )

    steps = CP // GROUP

    def along(t, y):
        c, p = t // steps, (t % steps) * GROUP
        hi, lo = [], []
        for q in range(GROUP):
            a_hi, a_lo = split2(cur[0, c, p + 1 + q, HALO : HALO + CS, :])
            b_hi, b_lo = split2(cur[1, c, p + 1 + q, HALO : HALO + CS, :])
            hi.append(jnp.concatenate([cast(a_hi), cast(b_hi)], axis=1))
            lo.append(jnp.concatenate([cast(a_lo), cast(b_lo)], axis=1))
        hi, lo = jnp.concatenate(hi, axis=0), jnp.concatenate(lo, axis=0)
        y[...] = dot_nn(hi, matrix) + dot_nn(lo, matrix)

    def finish(c, n, y):
        p = n * GROUP
        for q in range(GROUP):
            for h in range(2):
                up = cur[h, c, p + 1 + q, HALO + 1 : HALO + CS + 1, :]
                dn = cur[h, c, p + 1 + q, HALO - 1 : HALO + CS - 1, :]
                after = cur[h, c, p + 2 + q, HALO : HALO + CS, :]
                prior = cur[h, c, p + q, HALO : HALO + CS, :]
                mid = y[CS * q : CS * (q + 1), 128 * h : 128 * (h + 1)]
                value = 0.1 * (mid + (up + dn)) + (0.25 * prior - 0.05 * after)
                if c < 2 and h == 0:
                    wall = pltpu.roll(walls[...], 128 - (c * CP + p + q), 1)
                    value = value + jnp.where(first_lane, wall, 0.0)
                if c == 2 and h == 0:
                    kept[p + q, :, :] = value
                else:
                    work[h, c, p + q, :, :] = value

    for copy in loads[:2] + edges:
        copy.wait()
    along(0, y_even)
    for c in range(4):
        if c < 3:
            for copy in loads[2 * c + 2 : 2 * c + 4]:
                copy.wait()

        def body(n, _):
            t = c * steps + 2 * n
            along(t + 1, y_odd)
            finish(c, 2 * n, y_even)
            along(jnp.minimum(t + 2, 4 * steps - 1), y_even)
            finish(c, 2 * n + 1, y_odd)
            if c == 3:
                for h in range(2):
                    put(c, h, pl.ds(2 * n * GROUP, 2 * GROUP)).start()
            return 0

        lax.fori_loop(0, steps // 2, body, 0)
        if c < 3:
            for h in range(2):
                if c != 2 or h == 1:
                    put(c, h, pl.ds(0, CP)).start()
    for c in range(4):
        for h in range(2):
            if c != 2 or h == 1:
                put(c, h, pl.ds(0, CP)).wait()


def last_kernel(
    state, kept, recv, send, free, metal, owner, rank, top, coef, cell, wall_inv, metal_inv,
    out, metal_give,
    metal_out, sems,
):
    corner_f = 0.5 * wall_inv[0:1, 0:1]
    corner_m = 0.5 * metal_inv[0:1, 0:1]
    got = recv[...]
    from_owner = jnp.transpose(got)[0:32, :]
    parts = cast(jnp.concatenate(split3(from_owner), axis=0))
    total = jnp.zeros((CS, 96), F32)
    for b in range(FACES // FB):
        cols = slice(FB * b, FB * (b + 1))
        hot = jnp.where(iota((DEV, FB), 0) == owner[:, cols], 1.0, 0.0)
        y = dot_nn(parts, cast(hot))
        y = y[0:32, :] + y[32:64, :] + y[64:96, :]
        which = iota((CAP, FB), 0) == rank[:, cols]
        v0 = jnp.sum(jnp.where(which, y[0:16, :], 0.0), axis=0, keepdims=True)
        km = jnp.sum(jnp.where(which, y[16:32, :], 0.0), axis=0, keepdims=True)
        kf = coef[0:1, cols]
        p = top[:, cols]
        tw = (kf * p + km * v0) / (kf * (1.0 - corner_f) + km * (1.0 - corner_m))
        heat = kf * (p + (corner_f - 1.0) * tw)
        span_hot, pitch_hot = cell_tables(cell[:, cols])
        pieces = [jnp.where(pitch_hot, part, 0.0) for part in split3(heat)]
        total = total + dot_nt(cast(span_hot), cast(jnp.concatenate(pieces, axis=0)))
    wall = -0.5 * (total[:, 0:32] + total[:, 32:64] + total[:, 64:96])
    wall = jnp.concatenate([wall, jnp.zeros((CS, 96), F32)], axis=1)
    first_lane = iota((CS, 128), 1) == 0
    copies = []
    for p in range(CP):
        column = wall if p == 0 else pltpu.roll(wall, 128 - p, 1)
        kept[p] = kept[p] + jnp.where(first_lane, column, 0.0)
        if p % 16 == 15:
            planes = pl.ds(p - 15, 16)
            copies.append(
                pltpu.make_async_copy(
                    kept.at[planes], out.at[2, planes, :, pl.ds(0, 128)], sems.at[len(copies)]
                )
            )
            copies[-1].start()

    own = send[...]
    lane = iota((DEV, 128), 1)
    kf = pltpu.roll(got, 96, 1)
    p = pltpu.roll(got, 80, 1)
    km = pltpu.roll(own, 112, 1)
    valid = lane < CAP
    tw = (kf * p + km * own) / jnp.where(valid, kf * (1.0 - corner_f) + km * (1.0 - corner_m), 1.0)
    tw = jnp.where(valid, tw, 0.0)
    used = jnp.where(jnp.logical_and(valid, kf > 0.0), 1.0, 0.0)
    for step in (16, 32, 64):
        tw = tw + pltpu.roll(tw, step, 1)
        used = used + pltpu.roll(used, step, 1)
    mine = (lane >> 4) == (iota((DEV, 128), 0) & 7)
    tw = jnp.where(mine, tw, 0.0)
    used = jnp.where(mine, used, 0.0)
    gain = 0.5 * metal_inv[:, 0:1]
    for g in range(16):
        rows = slice(8 * g, 8 * g + 8)
        cols = slice(128 * g, 128 * g + 128)
        tw_row = jnp.sum(tw[rows, :], axis=0, keepdims=True)
        used_row = jnp.sum(used[rows, :], axis=0, keepdims=True)
        metal_out[:, cols] = jnp.where(
            used_row > 0.5, free[:, cols] + gain * tw_row, metal[:, cols]
        )
    copies.append(pltpu.make_async_copy(metal_out, metal_give, sems.at[2]))
    copies[-1].start()
    for copy in copies:
        copy.wait()


def spec(space):
    return pl.BlockSpec(memory_space=space)


ANY = pl.ANY
VM = pltpu.VMEM
HBM = pltpu.HBM


def shape(dims, dtype=F32):
    return jax.ShapeDtypeStruct(dims, dtype)


def params(limit=VMEM_LIMIT):
    return pltpu.CompilerParams(vmem_limit_bytes=limit)


def cost(microseconds):
    return pl.CostEstimate(
        flops=0, bytes_accessed=int(microseconds * 3_000_000), transcendentals=0
    )


def local(
    flow_state,
    wall_inverse,
    metal_inverse,
    metal_state,
    metal_conduct,
    face_coef,
    owner_map,
    face_cell,
    sample_col,
    sample_low,
):
    owner = owner_map.reshape(1, FACES)
    cell = face_cell.reshape(1, FACES)
    low = sample_low.reshape(1, FACES)
    conduct = metal_conduct.reshape(16, 128)
    send, give_pa, give_pb, give_sa, give_sb, rank, top, free, force = pl.pallas_call(
        first_kernel,
        name="first",
        in_specs=[spec(HBM)] * 10,
        out_specs=[spec(HBM)] * 5 + [spec(VM)] * 3 + [spec(HBM)],
        out_shape=[
            shape((DEV, 128)),
            shape((4, CS, GN)),
            shape((4, CS, GN)),
            shape((4, CP, GN)),
            shape((4, CP, GN)),
            shape((1, FACES), I32),
            shape((1, FACES)),
            shape((MP, SLOT_DEV)),
            shape((ROOM, FACES, 128)),
        ],
        scratch_shapes=[
            pltpu.VMEM((8, COLS + PAD, 128), F32),
            pltpu.VMEM((FACES, 128), I32),
            pltpu.VMEM((FACES, 128), F32),
            pltpu.VMEM((FACES, 128), F32),
            pltpu.VMEM((DEV, 128), F32),
            pltpu.VMEM((2, 4, CS, GN), F32),
            pltpu.VMEM((2, 4, CP, GN), F32),
            pltpu.SemaphoreType.DMA((12,)),
            pltpu.SMEM((FACES,), I32),
            pltpu.VMEM((1, FACES), I32),
            pltpu.VMEM((1, FACES), I32),
            pltpu.VMEM((2, FACES), F32),
            pltpu.VMEM((1, FACES), I32),
            pltpu.VMEM((WM, WM), F32),
            pltpu.VMEM((MP, MP), F32),
            pltpu.VMEM((MP, SLOT_DEV), F32),
            pltpu.VMEM((16, 128), F32),
        ],
        compiler_params=params(VMEM_WHOLE),
        cost_estimate=cost(7),
    )(
        flow_state, sample_col, low, owner, face_coef, cell, wall_inverse, metal_inverse,
        metal_state, conduct,
    )

    recv = lax.all_to_all(send, AXES, split_axis=0, concat_axis=0, tiled=True)

    n_pitch, n_span = lax.axis_size("pitch"), lax.axis_size("span")
    within_p = [(i, i ^ 1) for i in range(n_pitch)]
    across_p = [(i, (i + (1 if i & 1 else -1)) % n_pitch) for i in range(n_pitch)]
    within_s = [(i, i ^ 1) for i in range(n_span)]
    across_s = [(i, i + (1 if i & 1 else -1)) for i in range(1, n_span - 1)]
    got_pa = lax.ppermute(give_pa, "pitch", within_p)
    got_pb = lax.ppermute(give_pb, "pitch", across_p)
    got_sa = lax.ppermute(give_sa, "span", within_s)
    got_sb = lax.ppermute(give_sb, "span", across_s)

    new_state, kept = pl.pallas_call(
        stencil_kernel,
        name="stencil",
        in_specs=[spec(ANY), spec(ANY)] + [spec(VM)] * 3 + [spec(ANY)] * 2 + [spec(VM)] * 2,
        out_specs=[spec(ANY), spec(VM)],
        out_shape=[shape((4, CP, CS, GN)), shape((CP, CS, 128))],
        scratch_shapes=[
            pltpu.VMEM((2, 4, CP + 2, ROWS, 128), F32),
            pltpu.VMEM((2, 4, CP, CS, 128), F32),
            pltpu.VMEM((FACES, 128), F32),
            pltpu.VMEM((CS, 128), F32),
            pltpu.VMEM((GROUP * CS, GN), F32),
            pltpu.VMEM((GROUP * CS, GN), F32),
            pltpu.SemaphoreType.DMA((10,)),
        ],
        compiler_params=params(),
        cost_estimate=cost(10),
    )(flow_state, force, face_coef, cell, wall_inverse, got_pa, got_pb, got_sa, got_sb)

    new_state, metal_out = pl.pallas_call(
        last_kernel,
        name="last",
        in_specs=[spec(ANY)] + [spec(VM)] * 12,
        out_specs=[spec(ANY), spec(HBM)],
        out_shape=[shape((4, CP, CS, GN)), shape((MP, SLOT_DEV))],
        input_output_aliases={0: 0},
        scratch_shapes=[pltpu.VMEM((MP, SLOT_DEV), F32), pltpu.SemaphoreType.DMA((3,))],
        compiler_params=params(),
        cost_estimate=cost(3),
    )(
        new_state, kept, recv, send, free, metal_state, owner, rank, top, face_coef, cell,
        wall_inverse, metal_inverse,
    )
    return (new_state, metal_out)


def solution(mesh):
    return jax.shard_map(
        local,
        mesh=mesh,
        in_specs=(
            P(None, "pitch", "span", None),
            P(),
            P(),
            P(None, ("pitch", "span")),
            P(("pitch", "span")),
            P(None, ("pitch", "span")),
            P(("pitch", "span"), None),
            P(("pitch", "span")),
            P(("pitch", "span")),
            P(("pitch", "span")),
        ),
        out_specs=(P(None, "pitch", "span", None), P(None, ("pitch", "span"))),
        check_vma=False,
    )
```

```python
import jax
import jax.numpy as jnp
from jax import lax
from jax.experimental import pallas as pl
from jax.experimental.pallas import tpu as pltpu
from jax.sharding import PartitionSpec as P

CP = 32
CS = 64
GN = 256
WM = 64
MP = 16
CAP = 16
DEV = 128
FACES = 1024
SLOT_DEV = 2048
COLS = CP * CS
PICARD = 3

F32 = jnp.float32
BF16 = jnp.bfloat16
I32 = jnp.int32
AXES = ("pitch", "span")
VMEM_LIMIT = 48 * 1024 * 1024
VMEM_WHOLE = 60 * 1024 * 1024
FB = 256
PAD = 8
ROOM = 32


def iota(shape, dim):
    return lax.broadcasted_iota(I32, shape, dim)


def dot_nn(a, b):
    return lax.dot_general(a, b, (((1,), (0,)), ((), ())), preferred_element_type=F32)


def dot_nt(a, b):
    return lax.dot_general(a, b, (((1,), (1,)), ((), ())), preferred_element_type=F32)


def split2(x):
    hi = x.astype(BF16).astype(F32)
    return hi, x - hi


def split3(x):
    hi = x.astype(BF16).astype(F32)
    rest = x - hi
    mid = rest.astype(BF16).astype(F32)
    return hi, mid, rest - mid


def cast(x):
    return x.astype(BF16)


def cell_tables(cell_row):
    width = cell_row.shape[1]
    span_hot = iota((CS, width), 0) == (cell_row & (CS - 1))
    pitch_hot = iota((CP, width), 0) == (cell_row >> 6)
    return jnp.where(span_hot, 1.0, 0.0), pitch_hot


def gather_lane(source, index):
    return jnp.take_along_axis(source, index, axis=1)


def pick_rows(refs, col_ref, base):
    sub = iota((8, 128), 0)
    blocks = [None] * len(refs)
    for i in range(8):
        at = col_ref[base + i]
        for k, ref in enumerate(refs):
            row = jnp.broadcast_to(ref[pl.ds(at, 1), :], (8, 128))
            blocks[k] = row if i == 0 else jnp.where(sub == i, row, blocks[k])
    return blocks


def first_kernel(
    state, *args,
):
    sources, (send, give_pa, give_pb, give_sa, give_sb, rank, top, free, force_out) = args[:9], args[9:18]
    cur, lowb, temp, force, out_send, edge_p, edge_s, sems, *held = args[18:]
    col, low, owner, coef, cell, wall_inv, metal_inv, metal, conduct = held
    small = [
        pltpu.make_async_copy(source, target, sems.at[9 + (i == 0)])
        for i, (source, target) in enumerate(zip(sources, held))
    ]
    for copy in small:
        copy.start()
    odd_p, odd_s = lax.axis_index("pitch") & 1, lax.axis_index("span") & 1
    columns = state.reshape(4, COLS, GN)
    loads = []
    for i, c in enumerate((2, 0, 1, 3)):
        for h in range(2):
            loads.append(
                pltpu.make_async_copy(
                    columns.at[c, :, pl.ds(128 * h, 128)],
                    cur.at[2 * c + h, pl.ds(0, COLS)],
                    sems.at[i],
                )
            )
    for copy in loads[:6]:
        copy.start()
    edges_in = [
        pltpu.make_async_copy(state.at[:, (1 - odd_p) * (CP - 1)], edge_p.at[0], sems.at[4]),
        pltpu.make_async_copy(state.at[:, odd_p * (CP - 1)], edge_p.at[1], sems.at[5]),
    ]

    for copy in small[1:]:
        copy.wait()

    eye = iota((128, 128), 0) == iota((128, 128), 1)
    ones = jnp.ones((128, 128), BF16)
    low_f = low[...].astype(F32)
    for b in range(FACES // 128):
        diag = jnp.where(eye, low_f[:, 128 * b : 128 * (b + 1)], 0.0)
        lowb[pl.ds(128 * b, 128), :] = dot_nn(cast(diag), ones).astype(I32)

    m = metal[...]
    inv = metal_inv[...]
    v = inv[:, 0:1] * m[0:1, :]
    for j in range(1, MP):
        v = v + inv[:, j : j + 1] * m[j : j + 1, :]
    free[...] = v
    v0 = jnp.concatenate([v[0:1, 128 * g : 128 * (g + 1)] for g in range(16)], axis=0)
    spread = jnp.where((iota((DEV, 16), 0) >> 3) == iota((DEV, 16), 1), 1.0, 0.0)
    parts = jnp.concatenate(split3(v0) + split3(conduct[...]), axis=1)
    wide = dot_nn(cast(spread), cast(parts))
    lane = iota((DEV, 128), 1)
    mine = (lane >> 4) == (iota((DEV, 128), 0) & 7)
    folded = []
    for k in range(2):
        a = wide[:, 384 * k : 384 * (k + 1)]
        y = jnp.where(mine, a[:, 0:128] + a[:, 128:256] + a[:, 256:384], 0.0)
        for step in (64, 32, 16):
            y = y + pltpu.roll(y, step, 1)
        folded.append(y)
    own_half = jnp.where(lane < 16, folded[0], folded[1])

    before = jnp.where(iota((FB, FB), 0) < iota((FB, FB), 1), 1.0, 0.0).astype(BF16)
    carry = jnp.zeros((DEV, 1), F32)
    for b in range(FACES // FB):
        cols = slice(FB * b, FB * (b + 1))
        hot = jnp.where(iota((DEV, FB), 0) == owner[:, cols], 1.0, 0.0)
        prior = dot_nn(cast(hot), before) + carry
        carry = carry + jnp.sum(hot, axis=1, keepdims=True)
        rank[:, cols] = jnp.sum(hot * prior, axis=0, keepdims=True).astype(I32)

    small[0].wait()
    for copy in loads[:6]:
        copy.wait()
    for copy in loads[6:] + edges_in:
        copy.start()
    halves = [[cur.at[2 * c + h] for h in range(2)] for c in range(4)]
    lane8 = iota((8, 128), 1)
    left = lane8 < WM

    def body(g, _):
        base = g * 8
        index = lowb[pl.ds(base, 8), :] + (lane8 & (WM - 1))
        near = index < 128
        index = index & 127
        found = pick_rows([halves[c][h] for c in range(3) for h in range(2)], col, base)
        found = [gather_lane(x, index) for x in found]
        picked = [jnp.where(near, found[2 * c], found[2 * c + 1]) for c in range(3)]
        force[pl.ds(base, 8), :] = jnp.where(left, picked[0], picked[1])
        temp[pl.ds(base, 8), :] = picked[2]
        return 0

    lax.fori_loop(0, FACES // 8, body, 0, unroll=16)

    give = [pltpu.make_async_copy(force, force_out.at[0], sems.at[11])]
    give[0].start()

    for copy in loads[6:] + edges_in:
        copy.wait()
    edges_out = [
        pltpu.make_async_copy(edge_p.at[0], give_pa, sems.at[4]),
        pltpu.make_async_copy(edge_p.at[1], give_pb, sems.at[5]),
    ]
    for copy in edges_out:
        copy.start()
    for c in range(4):
        for h in range(2):
            lanes = slice(128 * h, 128 * h + 128)
            for p in range(0, CP, 8):
                for k, row in enumerate(((1 - odd_s) * (CS - 1), odd_s * (CS - 1))):
                    edge_s[k, c, p : p + 8, lanes] = halves[c][h][
                        pl.ds(p * CS + row, 8, stride=CS), :
                    ]
    give.append(pltpu.make_async_copy(edge_s.at[0], give_sa, sems.at[7]))
    give.append(pltpu.make_async_copy(edge_s.at[1], give_sb, sems.at[8]))
    give[-1].start()
    give[-2].start()

    g = wall_inv[...]
    g_hi, g_lo = split2(g)
    top_hi, top_lo = g_hi[0:1, :], g_lo[0:1, :]
    none = jnp.zeros((1, WM), F32)
    row16 = iota((16, 128), 0)
    query = jnp.where(
        row16 == 0,
        jnp.concatenate([top_hi, top_hi], axis=1),
        jnp.where(row16 == 1, jnp.concatenate([top_lo, none], axis=1), 0.0),
    )
    total = jnp.zeros((DEV, 128), F32)
    left_b = iota((FB, 128), 1) < WM
    for b in range(FACES // FB):
        cols = slice(FB * b, FB * (b + 1))
        x_hi, x_lo = split2(temp[cols, :])
        p = dot_nt(cast(query), cast(jnp.where(left_b, x_hi, x_lo)))
        p = p[0:1, :] + p[1:2, :]
        top[:, cols] = p
        hot = jnp.where(iota((DEV, FB), 0) == owner[:, cols], 1.0, 0.0)
        which = iota((CAP, FB), 0) == rank[:, cols]
        kf_parts = split3(coef[0:1, cols])
        p_parts = split3(p)
        pieces = [jnp.zeros((32, FB), F32)]
        for kf_part, p_part in zip(kf_parts, p_parts):
            pieces.append(jnp.where(which, kf_part, 0.0))
            pieces.append(jnp.where(which, p_part, 0.0))
        total = total + dot_nt(cast(hot), cast(jnp.concatenate(pieces, axis=0)))
    total = total + pltpu.roll(total, 96, 1) + pltpu.roll(total, 64, 1)
    out_send[...] = jnp.where(lane < 32, own_half, jnp.where(lane < 64, total, 0.0))
    give.append(pltpu.make_async_copy(out_send, send, sems.at[6]))
    give[-1].start()
    for copy in edges_out + give:
        copy.wait()


def drag(force, coef, cell, wall_inv, walls):
    g_hi, g_lo = split2(wall_inv[...])
    top_hi, top_lo = g_hi[0:1, :], g_lo[0:1, :]
    none = jnp.zeros((1, WM), F32)
    blank = jnp.zeros((WM, WM), F32)

    def twice(part):
        return jnp.concatenate(
            [
                jnp.concatenate([part, blank], axis=1),
                jnp.concatenate([blank, part], axis=1),
            ],
            axis=0,
        )

    both_hi = jnp.transpose(twice(g_hi))
    both_lo = jnp.transpose(twice(g_lo))
    table = cast(
        jnp.concatenate(
            [
                jnp.concatenate([both_hi, both_lo], axis=1),
                jnp.concatenate([both_hi, jnp.zeros_like(both_lo)], axis=1),
            ],
            axis=0,
        )
    )
    row16 = iota((16, 256), 0)
    picks = (
        jnp.concatenate([top_hi, none, top_hi, none], axis=1),
        jnp.concatenate([none, top_hi, none, top_hi], axis=1),
        jnp.concatenate([top_lo, none, none, none], axis=1),
        jnp.concatenate([none, top_lo, none, none], axis=1),
    )
    query = jnp.zeros((16, 256), F32)
    for i, pick in enumerate(picks):
        query = jnp.where(row16 == i, pick, query)
    query = cast(query)

    def packed(x):
        hi, lo = split2(x)
        return cast(jnp.concatenate([hi, lo], axis=1))

    blocks = [slice(FB * b, FB * (b + 1)) for b in range(FACES // FB)]
    ys = [dot_nn(packed(force[cols, :]), table) for cols in blocks]
    for step in range(PICARD):
        rhs = []
        for cols, y in zip(blocks, ys):
            x = y[:, :128] + y[:, 128:]
            sq = x * x
            damping = 0.5 * lax.rsqrt(1.0 + sq + pltpu.roll(sq, WM, 1))
            rhs.append(packed(force[cols, :] - damping * x))
        if step < PICARD - 1:
            ys = [dot_nn(r, table) for r in rhs]
        else:
            ys = [dot_nt(query, r) for r in rhs]
    total = jnp.zeros((CS, 192), F32)
    for cols, y in zip(blocks, ys):
        nu = coef[1:2, cols]
        flux_u = nu * (y[0:1, :] + y[2:3, :])
        flux_w = nu * (y[1:2, :] + y[3:4, :])
        span_hot, pitch_hot = cell_tables(cell[:, cols])
        pieces = []
        for u_part, w_part in zip(split3(flux_u), split3(flux_w)):
            pieces.append(jnp.where(pitch_hot, u_part, 0.0))
            pieces.append(jnp.where(pitch_hot, w_part, 0.0))
        total = total + dot_nt(cast(span_hot), cast(jnp.concatenate(pieces, axis=0)))
    walls[...] = jnp.zeros((CS, 128), F32)
    walls[:, 0:64] = -0.5 * (total[:, 0:64] + total[:, 64:128] + total[:, 128:192])


GROUP = 4
HALO = 8
ROWS = CS + 2 * HALO


def stencil_kernel(
    state, force_in, coef, cell, wall_inv, got_pa, got_pb, got_sa, got_sb,
    out, kept,
    cur, work, force, walls, y_even, y_odd, sems,
):
    odd_p, odd_s = lax.axis_index("pitch") & 1, lax.axis_index("span") & 1
    inner = pl.ds(HALO, CS)
    bring = pltpu.make_async_copy(force_in.at[0], force, sems.at[9])
    bring.start()
    loads = []
    for c in range(4):
        for h in range(2):
            lanes = pl.ds(128 * h, 128)
            loads.append(
                pltpu.make_async_copy(
                    state.at[c, :, :, lanes], cur.at[h, c, pl.ds(1, CP), inner, :], sems.at[c]
                )
            )
    edges = []
    for h in range(2):
        lanes = pl.ds(128 * h, 128)
        for plane, source in (((1 - odd_p) * (CP + 1), got_pa), (odd_p * (CP + 1), got_pb)):
            edges.append(
                pltpu.make_async_copy(
                    source.at[:, :, lanes], cur.at[h, :, plane, inner, :], sems.at[4]
                )
            )
    for copy in loads[:2] + edges + loads[2:]:
        copy.start()

    flat = cur.reshape(2 * 4 * (CP + 2) * ROWS, 128)
    below, above = HALO - 1, HALO + CS
    row_a = above + odd_s * (below - above)
    row_b = below + odd_s * (above - below)
    for h in range(2):
        lanes = slice(128 * h, 128 * h + 128)
        for c in range(4):
            for p in range(0, CP, 8):
                start = ((h * 4 + c) * (CP + 2) + 1 + p) * ROWS
                flat[pl.ds(start + row_a, 8, stride=ROWS), :] = got_sa[c, p : p + 8, lanes]
                flat[pl.ds(start + row_b, 8, stride=ROWS), :] = got_sb[c, p : p + 8, lanes]

    bring.wait()
    drag(force, coef, cell, wall_inv, walls)

    i, j = iota((GN, GN), 0), iota((GN, GN), 1)
    near = jnp.where(jnp.abs(i - j) == 1, 1.0, 0.0)
    same = jnp.where((i == 0) | (i == GN - 1), 5.0, 4.0)
    matrix = cast(jnp.where(i == j, same, near))
    first_lane = iota((CS, 128), 1) == 0

    def put(c, h, planes):
        lanes = pl.ds(128 * h, 128)
        return pltpu.make_async_copy(
            work.at[h, c, planes], out.at[c, planes, :, lanes], sems.at[5 + c]
        )

    steps = CP // GROUP

    def along(t, y):
        c, p = t // steps, (t % steps) * GROUP
        hi, lo = [], []
        for q in range(GROUP):
            a_hi, a_lo = split2(cur[0, c, p + 1 + q, HALO : HALO + CS, :])
            b_hi, b_lo = split2(cur[1, c, p + 1 + q, HALO : HALO + CS, :])
            hi.append(jnp.concatenate([cast(a_hi), cast(b_hi)], axis=1))
            lo.append(jnp.concatenate([cast(a_lo), cast(b_lo)], axis=1))
        hi, lo = jnp.concatenate(hi, axis=0), jnp.concatenate(lo, axis=0)
        y[...] = dot_nn(hi, matrix) + dot_nn(lo, matrix)

    def finish(c, n, y):
        p = n * GROUP
        for q in range(GROUP):
            for h in range(2):
                up = cur[h, c, p + 1 + q, HALO + 1 : HALO + CS + 1, :]
                dn = cur[h, c, p + 1 + q, HALO - 1 : HALO + CS - 1, :]
                after = cur[h, c, p + 2 + q, HALO : HALO + CS, :]
                prior = cur[h, c, p + q, HALO : HALO + CS, :]
                mid = y[CS * q : CS * (q + 1), 128 * h : 128 * (h + 1)]
                value = 0.1 * (mid + (up + dn)) + (0.25 * prior - 0.05 * after)
                if c < 2 and h == 0:
                    wall = pltpu.roll(walls[...], 128 - (c * CP + p + q), 1)
                    value = value + jnp.where(first_lane, wall, 0.0)
                if c == 2 and h == 0:
                    kept[p + q, :, :] = value
                else:
                    work[h, c, p + q, :, :] = value

    for copy in loads[:2] + edges:
        copy.wait()
    along(0, y_even)
    for c in range(4):
        if c < 3:
            for copy in loads[2 * c + 2 : 2 * c + 4]:
                copy.wait()

        def body(n, _):
            t = c * steps + 2 * n
            along(t + 1, y_odd)
            finish(c, 2 * n, y_even)
            along(jnp.minimum(t + 2, 4 * steps - 1), y_even)
            finish(c, 2 * n + 1, y_odd)
            if c == 3:
                for h in range(2):
                    put(c, h, pl.ds(2 * n * GROUP, 2 * GROUP)).start()
            return 0

        lax.fori_loop(0, steps // 2, body, 0)
        if c < 3:
            for h in range(2):
                if c != 2 or h == 1:
                    put(c, h, pl.ds(0, CP)).start()
    for c in range(4):
        for h in range(2):
            if c != 2 or h == 1:
                put(c, h, pl.ds(0, CP)).wait()


def last_kernel(
    state, kept, recv, send, free, metal, owner, rank, top, coef, cell, wall_inv, metal_inv,
    out, metal_give,
    metal_out, sems,
):
    corner_f = 0.5 * wall_inv[0:1, 0:1]
    corner_m = 0.5 * metal_inv[0:1, 0:1]
    got = recv[...]
    from_owner = jnp.transpose(got)[0:32, :]
    parts = cast(jnp.concatenate(split3(from_owner), axis=0))
    total = jnp.zeros((CS, 96), F32)
    for b in range(FACES // FB):
        cols = slice(FB * b, FB * (b + 1))
        hot = jnp.where(iota((DEV, FB), 0) == owner[:, cols], 1.0, 0.0)
        y = dot_nn(parts, cast(hot))
        y = y[0:32, :] + y[32:64, :] + y[64:96, :]
        which = iota((CAP, FB), 0) == rank[:, cols]
        v0 = jnp.sum(jnp.where(which, y[0:16, :], 0.0), axis=0, keepdims=True)
        km = jnp.sum(jnp.where(which, y[16:32, :], 0.0), axis=0, keepdims=True)
        kf = coef[0:1, cols]
        p = top[:, cols]
        tw = (kf * p + km * v0) / (kf * (1.0 - corner_f) + km * (1.0 - corner_m))
        heat = kf * (p + (corner_f - 1.0) * tw)
        span_hot, pitch_hot = cell_tables(cell[:, cols])
        pieces = [jnp.where(pitch_hot, part, 0.0) for part in split3(heat)]
        total = total + dot_nt(cast(span_hot), cast(jnp.concatenate(pieces, axis=0)))
    wall = -0.5 * (total[:, 0:32] + total[:, 32:64] + total[:, 64:96])
    wall = jnp.concatenate([wall, jnp.zeros((CS, 96), F32)], axis=1)
    first_lane = iota((CS, 128), 1) == 0
    copies = []
    for p in range(CP):
        column = wall if p == 0 else pltpu.roll(wall, 128 - p, 1)
        kept[p] = kept[p] + jnp.where(first_lane, column, 0.0)
        if p % 16 == 15:
            planes = pl.ds(p - 15, 16)
            copies.append(
                pltpu.make_async_copy(
                    kept.at[planes], out.at[2, planes, :, pl.ds(0, 128)], sems.at[len(copies)]
                )
            )
            copies[-1].start()

    own = send[...]
    lane = iota((DEV, 128), 1)
    kf = pltpu.roll(got, 96, 1)
    p = pltpu.roll(got, 80, 1)
    km = pltpu.roll(own, 112, 1)
    valid = lane < CAP
    tw = (kf * p + km * own) / jnp.where(valid, kf * (1.0 - corner_f) + km * (1.0 - corner_m), 1.0)
    tw = jnp.where(valid, tw, 0.0)
    used = jnp.where(jnp.logical_and(valid, kf > 0.0), 1.0, 0.0)
    for step in (16, 32, 64):
        tw = tw + pltpu.roll(tw, step, 1)
        used = used + pltpu.roll(used, step, 1)
    mine = (lane >> 4) == (iota((DEV, 128), 0) & 7)
    tw = jnp.where(mine, tw, 0.0)
    used = jnp.where(mine, used, 0.0)
    gain = 0.5 * metal_inv[:, 0:1]
    for g in range(16):
        rows = slice(8 * g, 8 * g + 8)
        cols = slice(128 * g, 128 * g + 128)
        tw_row = jnp.sum(tw[rows, :], axis=0, keepdims=True)
        used_row = jnp.sum(used[rows, :], axis=0, keepdims=True)
        metal_out[:, cols] = jnp.where(
            used_row > 0.5, free[:, cols] + gain * tw_row, metal[:, cols]
        )
    copies.append(pltpu.make_async_copy(metal_out, metal_give, sems.at[2]))
    copies[-1].start()
    for copy in copies:
        copy.wait()


def spec(space):
    return pl.BlockSpec(memory_space=space)


ANY = pl.ANY
VM = pltpu.VMEM
HBM = pltpu.HBM


def shape(dims, dtype=F32):
    return jax.ShapeDtypeStruct(dims, dtype)


def params(limit=VMEM_LIMIT):
    return pltpu.CompilerParams(vmem_limit_bytes=limit)


def cost(microseconds):
    return pl.CostEstimate(
        flops=0, bytes_accessed=int(microseconds * 3_000_000), transcendentals=0
    )


def local(
    flow_state,
    wall_inverse,
    metal_inverse,
    metal_state,
    metal_conduct,
    face_coef,
    owner_map,
    face_cell,
    sample_col,
    sample_low,
):
    owner = owner_map.reshape(1, FACES)
    cell = face_cell.reshape(1, FACES)
    low = sample_low.reshape(1, FACES)
    conduct = metal_conduct.reshape(16, 128)
    send, give_pa, give_pb, give_sa, give_sb, rank, top, free, force = pl.pallas_call(
        first_kernel,
        name="first",
        in_specs=[spec(HBM)] * 10,
        out_specs=[spec(HBM)] * 5 + [spec(VM)] * 3 + [spec(HBM)],
        out_shape=[
            shape((DEV, 128)),
            shape((4, CS, GN)),
            shape((4, CS, GN)),
            shape((4, CP, GN)),
            shape((4, CP, GN)),
            shape((1, FACES), I32),
            shape((1, FACES)),
            shape((MP, SLOT_DEV)),
            shape((ROOM, FACES, 128)),
        ],
        scratch_shapes=[
            pltpu.VMEM((8, COLS + PAD, 128), F32),
            pltpu.VMEM((FACES, 128), I32),
            pltpu.VMEM((FACES, 128), F32),
            pltpu.VMEM((FACES, 128), F32),
            pltpu.VMEM((DEV, 128), F32),
            pltpu.VMEM((2, 4, CS, GN), F32),
            pltpu.VMEM((2, 4, CP, GN), F32),
            pltpu.SemaphoreType.DMA((12,)),
            pltpu.SMEM((FACES,), I32),
            pltpu.VMEM((1, FACES), I32),
            pltpu.VMEM((1, FACES), I32),
            pltpu.VMEM((2, FACES), F32),
            pltpu.VMEM((1, FACES), I32),
            pltpu.VMEM((WM, WM), F32),
            pltpu.VMEM((MP, MP), F32),
            pltpu.VMEM((MP, SLOT_DEV), F32),
            pltpu.VMEM((16, 128), F32),
        ],
        compiler_params=params(VMEM_WHOLE),
        cost_estimate=cost(7),
    )(
        flow_state, sample_col, low, owner, face_coef, cell, wall_inverse, metal_inverse,
        metal_state, conduct,
    )

    recv = lax.all_to_all(send, AXES, split_axis=0, concat_axis=0, tiled=True)

    n_pitch, n_span = lax.axis_size("pitch"), lax.axis_size("span")
    within_p = [(i, i ^ 1) for i in range(n_pitch)]
    across_p = [(i, (i + (1 if i & 1 else -1)) % n_pitch) for i in range(n_pitch)]
    within_s = [(i, i ^ 1) for i in range(n_span)]
    across_s = [(i, i + (1 if i & 1 else -1)) for i in range(1, n_span - 1)]
    got_pa = lax.ppermute(give_pa, "pitch", within_p)
    got_pb = lax.ppermute(give_pb, "pitch", across_p)
    got_sa = lax.ppermute(give_sa, "span", within_s)
    got_sb = lax.ppermute(give_sb, "span", across_s)

    new_state, kept = pl.pallas_call(
        stencil_kernel,
        name="stencil",
        in_specs=[spec(ANY), spec(ANY)] + [spec(VM)] * 3 + [spec(ANY)] * 2 + [spec(VM)] * 2,
        out_specs=[spec(ANY), spec(VM)],
        out_shape=[shape((4, CP, CS, GN)), shape((CP, CS, 128))],
        scratch_shapes=[
            pltpu.VMEM((2, 4, CP + 2, ROWS, 128), F32),
            pltpu.VMEM((2, 4, CP, CS, 128), F32),
            pltpu.VMEM((FACES, 128), F32),
            pltpu.VMEM((CS, 128), F32),
            pltpu.VMEM((GROUP * CS, GN), F32),
            pltpu.VMEM((GROUP * CS, GN), F32),
            pltpu.SemaphoreType.DMA((10,)),
        ],
        compiler_params=params(),
        cost_estimate=cost(10),
    )(flow_state, force, face_coef, cell, wall_inverse, got_pa, got_pb, got_sa, got_sb)

    new_state, metal_out = pl.pallas_call(
        last_kernel,
        name="last",
        in_specs=[spec(ANY)] + [spec(VM)] * 12,
        out_specs=[spec(ANY), spec(HBM)],
        out_shape=[shape((4, CP, CS, GN)), shape((MP, SLOT_DEV))],
        input_output_aliases={0: 0},
        scratch_shapes=[pltpu.VMEM((MP, SLOT_DEV), F32), pltpu.SemaphoreType.DMA((3,))],
        compiler_params=params(),
        cost_estimate=cost(3),
    )(
        new_state, kept, recv, send, free, metal_state, owner, rank, top, face_coef, cell,
        wall_inverse, metal_inverse,
    )
    return (new_state, metal_out)


def solution(mesh):
    return jax.shard_map(
        local,
        mesh=mesh,
        in_specs=(
            P(None, "pitch", "span", None),
            P(),
            P(),
            P(None, ("pitch", "span")),
            P(("pitch", "span")),
            P(None, ("pitch", "span")),
            P(("pitch", "span"), None),
            P(("pitch", "span")),
            P(("pitch", "span")),
            P(("pitch", "span")),
        ),
        out_specs=(P(None, "pitch", "span", None), P(None, ("pitch", "span"))),
        check_vma=False,
    )
```

```python
import jax
import jax.numpy as jnp
from jax import lax
from jax.experimental import pallas as pl
from jax.experimental.pallas import tpu as pltpu
from jax.sharding import PartitionSpec as P

CP = 32
CS = 64
GN = 256
WM = 64
MP = 16
CAP = 16
DEV = 128
FACES = 1024
SLOT_DEV = 2048
COLS = CP * CS
PICARD = 3

F32 = jnp.float32
BF16 = jnp.bfloat16
I32 = jnp.int32
AXES = ("pitch", "span")
VMEM_LIMIT = 48 * 1024 * 1024
VMEM_WHOLE = 60 * 1024 * 1024
FB = 256
PAD = 8
ROOM = 32


def iota(shape, dim):
    return lax.broadcasted_iota(I32, shape, dim)


def dot_nn(a, b):
    return lax.dot_general(a, b, (((1,), (0,)), ((), ())), preferred_element_type=F32)


def dot_nt(a, b):
    return lax.dot_general(a, b, (((1,), (1,)), ((), ())), preferred_element_type=F32)


def split2(x):
    hi = x.astype(BF16).astype(F32)
    return hi, x - hi


def split3(x):
    hi = x.astype(BF16).astype(F32)
    rest = x - hi
    mid = rest.astype(BF16).astype(F32)
    return hi, mid, rest - mid


def cast(x):
    return x.astype(BF16)


def cell_tables(cell_row):
    width = cell_row.shape[1]
    span_hot = iota((CS, width), 0) == (cell_row & (CS - 1))
    pitch_hot = iota((CP, width), 0) == (cell_row >> 6)
    return jnp.where(span_hot, 1.0, 0.0), pitch_hot


def gather_lane(source, index):
    return jnp.take_along_axis(source, index, axis=1)


def pick_rows(refs, col_ref, base):
    sub = iota((8, 128), 0)
    blocks = [None] * len(refs)
    for i in range(8):
        at = col_ref[base + i]
        for k, ref in enumerate(refs):
            row = jnp.broadcast_to(ref[pl.ds(at, 1), :], (8, 128))
            blocks[k] = row if i == 0 else jnp.where(sub == i, row, blocks[k])
    return blocks


def first_kernel(
    state, *args,
):
    sources, (send, give_pa, give_pb, give_sa, give_sb, rank, top, free, force_out) = args[:9], args[9:18]
    cur, lowb, temp, force, out_send, edge_p, edge_s, sems, *held = args[18:]
    col, low, owner, coef, cell, wall_inv, metal_inv, metal, conduct = held
    small = [
        pltpu.make_async_copy(source, target, sems.at[9 + (i == 0)])
        for i, (source, target) in enumerate(zip(sources, held))
    ]
    for copy in small:
        copy.start()
    odd_p, odd_s = lax.axis_index("pitch") & 1, lax.axis_index("span") & 1
    columns = state.reshape(4, COLS, GN)
    loads = []
    for i, c in enumerate((2, 0, 1, 3)):
        for h in range(2):
            loads.append(
                pltpu.make_async_copy(
                    columns.at[c, :, pl.ds(128 * h, 128)],
                    cur.at[2 * c + h, pl.ds(0, COLS)],
                    sems.at[i],
                )
            )
    for copy in loads[:6]:
        copy.start()
    edges_in = [
        pltpu.make_async_copy(state.at[:, (1 - odd_p) * (CP - 1)], edge_p.at[0], sems.at[4]),
        pltpu.make_async_copy(state.at[:, odd_p * (CP - 1)], edge_p.at[1], sems.at[5]),
    ]

    for copy in small[1:]:
        copy.wait()

    eye = iota((128, 128), 0) == iota((128, 128), 1)
    ones = jnp.ones((128, 128), BF16)
    low_f = low[...].astype(F32)
    for b in range(FACES // 128):
        diag = jnp.where(eye, low_f[:, 128 * b : 128 * (b + 1)], 0.0)
        lowb[pl.ds(128 * b, 128), :] = dot_nn(cast(diag), ones).astype(I32)

    m = metal[...]
    inv = metal_inv[...]
    v = inv[:, 0:1] * m[0:1, :]
    for j in range(1, MP):
        v = v + inv[:, j : j + 1] * m[j : j + 1, :]
    free[...] = v
    v0 = jnp.concatenate([v[0:1, 128 * g : 128 * (g + 1)] for g in range(16)], axis=0)
    spread = jnp.where((iota((DEV, 16), 0) >> 3) == iota((DEV, 16), 1), 1.0, 0.0)
    parts = jnp.concatenate(split3(v0) + split3(conduct[...]), axis=1)
    wide = dot_nn(cast(spread), cast(parts))
    lane = iota((DEV, 128), 1)
    mine = (lane >> 4) == (iota((DEV, 128), 0) & 7)
    folded = []
    for k in range(2):
        a = wide[:, 384 * k : 384 * (k + 1)]
        y = jnp.where(mine, a[:, 0:128] + a[:, 128:256] + a[:, 256:384], 0.0)
        for step in (64, 32, 16):
            y = y + pltpu.roll(y, step, 1)
        folded.append(y)
    own_half = jnp.where(lane < 16, folded[0], folded[1])

    before = jnp.where(iota((FB, FB), 0) < iota((FB, FB), 1), 1.0, 0.0).astype(BF16)
    carry = jnp.zeros((DEV, 1), F32)
    for b in range(FACES // FB):
        cols = slice(FB * b, FB * (b + 1))
        hot = jnp.where(iota((DEV, FB), 0) == owner[:, cols], 1.0, 0.0)
        prior = dot_nn(cast(hot), before) + carry
        carry = carry + jnp.sum(hot, axis=1, keepdims=True)
        rank[:, cols] = jnp.sum(hot * prior, axis=0, keepdims=True).astype(I32)

    small[0].wait()
    for copy in loads[:6]:
        copy.wait()
    for copy in loads[6:] + edges_in:
        copy.start()
    halves = [[cur.at[2 * c + h] for h in range(2)] for c in range(4)]
    lane8 = iota((8, 128), 1)
    left = lane8 < WM

    def body(g, _):
        base = g * 8
        index = lowb[pl.ds(base, 8), :] + (lane8 & (WM - 1))
        near = index < 128
        index = index & 127
        found = pick_rows([halves[c][h] for c in range(3) for h in range(2)], col, base)
        found = [gather_lane(x, index) for x in found]
        picked = [jnp.where(near, found[2 * c], found[2 * c + 1]) for c in range(3)]
        force[pl.ds(base, 8), :] = jnp.where(left, picked[0], picked[1])
        temp[pl.ds(base, 8), :] = picked[2]
        return 0

    lax.fori_loop(0, FACES // 8, body, 0, unroll=32)

    give = [pltpu.make_async_copy(force, force_out.at[0], sems.at[11])]
    give[0].start()

    for copy in loads[6:] + edges_in:
        copy.wait()
    edges_out = [
        pltpu.make_async_copy(edge_p.at[0], give_pa, sems.at[4]),
        pltpu.make_async_copy(edge_p.at[1], give_pb, sems.at[5]),
    ]
    for copy in edges_out:
        copy.start()
    for c in range(4):
        for h in range(2):
            lanes = slice(128 * h, 128 * h + 128)
            for p in range(0, CP, 8):
                for k, row in enumerate(((1 - odd_s) * (CS - 1), odd_s * (CS - 1))):
                    edge_s[k, c, p : p + 8, lanes] = halves[c][h][
                        pl.ds(p * CS + row, 8, stride=CS), :
                    ]
    give.append(pltpu.make_async_copy(edge_s.at[0], give_sa, sems.at[7]))
    give.append(pltpu.make_async_copy(edge_s.at[1], give_sb, sems.at[8]))
    give[-1].start()
    give[-2].start()

    g = wall_inv[...]
    g_hi, g_lo = split2(g)
    top_hi, top_lo = g_hi[0:1, :], g_lo[0:1, :]
    none = jnp.zeros((1, WM), F32)
    row16 = iota((16, 128), 0)
    query = jnp.where(
        row16 == 0,
        jnp.concatenate([top_hi, top_hi], axis=1),
        jnp.where(row16 == 1, jnp.concatenate([top_lo, none], axis=1), 0.0),
    )
    total = jnp.zeros((DEV, 128), F32)
    left_b = iota((FB, 128), 1) < WM
    for b in range(FACES // FB):
        cols = slice(FB * b, FB * (b + 1))
        x_hi, x_lo = split2(temp[cols, :])
        p = dot_nt(cast(query), cast(jnp.where(left_b, x_hi, x_lo)))
        p = p[0:1, :] + p[1:2, :]
        top[:, cols] = p
        hot = jnp.where(iota((DEV, FB), 0) == owner[:, cols], 1.0, 0.0)
        which = iota((CAP, FB), 0) == rank[:, cols]
        kf_parts = split3(coef[0:1, cols])
        p_parts = split3(p)
        pieces = [jnp.zeros((32, FB), F32)]
        for kf_part, p_part in zip(kf_parts, p_parts):
            pieces.append(jnp.where(which, kf_part, 0.0))
            pieces.append(jnp.where(which, p_part, 0.0))
        total = total + dot_nt(cast(hot), cast(jnp.concatenate(pieces, axis=0)))
    total = total + pltpu.roll(total, 96, 1) + pltpu.roll(total, 64, 1)
    out_send[...] = jnp.where(lane < 32, own_half, jnp.where(lane < 64, total, 0.0))
    give.append(pltpu.make_async_copy(out_send, send, sems.at[6]))
    give[-1].start()
    for copy in edges_out + give:
        copy.wait()


def drag(force, coef, cell, wall_inv, walls):
    g_hi, g_lo = split2(wall_inv[...])
    top_hi, top_lo = g_hi[0:1, :], g_lo[0:1, :]
    none = jnp.zeros((1, WM), F32)
    blank = jnp.zeros((WM, WM), F32)

    def twice(part):
        return jnp.concatenate(
            [
                jnp.concatenate([part, blank], axis=1),
                jnp.concatenate([blank, part], axis=1),
            ],
            axis=0,
        )

    both_hi = jnp.transpose(twice(g_hi))
    both_lo = jnp.transpose(twice(g_lo))
    table = cast(
        jnp.concatenate(
            [
                jnp.concatenate([both_hi, both_lo], axis=1),
                jnp.concatenate([both_hi, jnp.zeros_like(both_lo)], axis=1),
            ],
            axis=0,
        )
    )
    row16 = iota((16, 256), 0)
    picks = (
        jnp.concatenate([top_hi, none, top_hi, none], axis=1),
        jnp.concatenate([none, top_hi, none, top_hi], axis=1),
        jnp.concatenate([top_lo, none, none, none], axis=1),
        jnp.concatenate([none, top_lo, none, none], axis=1),
    )
    query = jnp.zeros((16, 256), F32)
    for i, pick in enumerate(picks):
        query = jnp.where(row16 == i, pick, query)
    query = cast(query)

    def packed(x):
        hi, lo = split2(x)
        return cast(jnp.concatenate([hi, lo], axis=1))

    blocks = [slice(FB * b, FB * (b + 1)) for b in range(FACES // FB)]
    ys = [dot_nn(packed(force[cols, :]), table) for cols in blocks]
    for step in range(PICARD):
        rhs = []
        for cols, y in zip(blocks, ys):
            x = y[:, :128] + y[:, 128:]
            sq = x * x
            damping = 0.5 * lax.rsqrt(1.0 + sq + pltpu.roll(sq, WM, 1))
            rhs.append(packed(force[cols, :] - damping * x))
        if step < PICARD - 1:
            ys = [dot_nn(r, table) for r in rhs]
        else:
            ys = [dot_nt(query, r) for r in rhs]
    total = jnp.zeros((CS, 192), F32)
    for cols, y in zip(blocks, ys):
        nu = coef[1:2, cols]
        flux_u = nu * (y[0:1, :] + y[2:3, :])
        flux_w = nu * (y[1:2, :] + y[3:4, :])
        span_hot, pitch_hot = cell_tables(cell[:, cols])
        pieces = []
        for u_part, w_part in zip(split3(flux_u), split3(flux_w)):
            pieces.append(jnp.where(pitch_hot, u_part, 0.0))
            pieces.append(jnp.where(pitch_hot, w_part, 0.0))
        total = total + dot_nt(cast(span_hot), cast(jnp.concatenate(pieces, axis=0)))
    walls[...] = jnp.zeros((CS, 128), F32)
    walls[:, 0:64] = -0.5 * (total[:, 0:64] + total[:, 64:128] + total[:, 128:192])


GROUP = 4
HALO = 8
ROWS = CS + 2 * HALO


def stencil_kernel(
    state, force_in, coef, cell, wall_inv, got_pa, got_pb, got_sa, got_sb,
    out, kept,
    cur, work, force, walls, y_even, y_odd, sems,
):
    odd_p, odd_s = lax.axis_index("pitch") & 1, lax.axis_index("span") & 1
    inner = pl.ds(HALO, CS)
    bring = pltpu.make_async_copy(force_in.at[0], force, sems.at[9])
    bring.start()
    loads = []
    for c in range(4):
        for h in range(2):
            lanes = pl.ds(128 * h, 128)
            loads.append(
                pltpu.make_async_copy(
                    state.at[c, :, :, lanes], cur.at[h, c, pl.ds(1, CP), inner, :], sems.at[c]
                )
            )
    edges = []
    for h in range(2):
        lanes = pl.ds(128 * h, 128)
        for plane, source in (((1 - odd_p) * (CP + 1), got_pa), (odd_p * (CP + 1), got_pb)):
            edges.append(
                pltpu.make_async_copy(
                    source.at[:, :, lanes], cur.at[h, :, plane, inner, :], sems.at[4]
                )
            )
    for copy in loads[:2] + edges + loads[2:]:
        copy.start()

    flat = cur.reshape(2 * 4 * (CP + 2) * ROWS, 128)
    below, above = HALO - 1, HALO + CS
    row_a = above + odd_s * (below - above)
    row_b = below + odd_s * (above - below)
    for h in range(2):
        lanes = slice(128 * h, 128 * h + 128)
        for c in range(4):
            for p in range(0, CP, 8):
                start = ((h * 4 + c) * (CP + 2) + 1 + p) * ROWS
                flat[pl.ds(start + row_a, 8, stride=ROWS), :] = got_sa[c, p : p + 8, lanes]
                flat[pl.ds(start + row_b, 8, stride=ROWS), :] = got_sb[c, p : p + 8, lanes]

    bring.wait()
    drag(force, coef, cell, wall_inv, walls)

    i, j = iota((GN, GN), 0), iota((GN, GN), 1)
    near = jnp.where(jnp.abs(i - j) == 1, 1.0, 0.0)
    same = jnp.where((i == 0) | (i == GN - 1), 5.0, 4.0)
    matrix = cast(jnp.where(i == j, same, near))
    first_lane = iota((CS, 128), 1) == 0

    def put(c, h, planes):
        lanes = pl.ds(128 * h, 128)
        return pltpu.make_async_copy(
            work.at[h, c, planes], out.at[c, planes, :, lanes], sems.at[5 + c]
        )

    steps = CP // GROUP

    def along(t, y):
        c, p = t // steps, (t % steps) * GROUP
        hi, lo = [], []
        for q in range(GROUP):
            a_hi, a_lo = split2(cur[0, c, p + 1 + q, HALO : HALO + CS, :])
            b_hi, b_lo = split2(cur[1, c, p + 1 + q, HALO : HALO + CS, :])
            hi.append(jnp.concatenate([cast(a_hi), cast(b_hi)], axis=1))
            lo.append(jnp.concatenate([cast(a_lo), cast(b_lo)], axis=1))
        hi, lo = jnp.concatenate(hi, axis=0), jnp.concatenate(lo, axis=0)
        y[...] = dot_nn(hi, matrix) + dot_nn(lo, matrix)

    def finish(c, n, y):
        p = n * GROUP
        for q in range(GROUP):
            for h in range(2):
                up = cur[h, c, p + 1 + q, HALO + 1 : HALO + CS + 1, :]
                dn = cur[h, c, p + 1 + q, HALO - 1 : HALO + CS - 1, :]
                after = cur[h, c, p + 2 + q, HALO : HALO + CS, :]
                prior = cur[h, c, p + q, HALO : HALO + CS, :]
                mid = y[CS * q : CS * (q + 1), 128 * h : 128 * (h + 1)]
                value = 0.1 * (mid + (up + dn)) + (0.25 * prior - 0.05 * after)
                if c < 2 and h == 0:
                    wall = pltpu.roll(walls[...], 128 - (c * CP + p + q), 1)
                    value = value + jnp.where(first_lane, wall, 0.0)
                if c == 2 and h == 0:
                    kept[p + q, :, :] = value
                else:
                    work[h, c, p + q, :, :] = value

    for copy in loads[:2] + edges:
        copy.wait()
    along(0, y_even)
    for c in range(4):
        if c < 3:
            for copy in loads[2 * c + 2 : 2 * c + 4]:
                copy.wait()

        def body(n, _):
            t = c * steps + 2 * n
            along(t + 1, y_odd)
            finish(c, 2 * n, y_even)
            along(jnp.minimum(t + 2, 4 * steps - 1), y_even)
            finish(c, 2 * n + 1, y_odd)
            if c == 3:
                for h in range(2):
                    put(c, h, pl.ds(2 * n * GROUP, 2 * GROUP)).start()
            return 0

        lax.fori_loop(0, steps // 2, body, 0)
        if c < 3:
            for h in range(2):
                if c != 2 or h == 1:
                    put(c, h, pl.ds(0, CP)).start()
    for c in range(4):
        for h in range(2):
            if c != 2 or h == 1:
                put(c, h, pl.ds(0, CP)).wait()


def last_kernel(
    state, kept, recv, send, free, metal, owner, rank, top, coef, cell, wall_inv, metal_inv,
    out, metal_give,
    metal_out, sems,
):
    corner_f = 0.5 * wall_inv[0:1, 0:1]
    corner_m = 0.5 * metal_inv[0:1, 0:1]
    got = recv[...]
    from_owner = jnp.transpose(got)[0:32, :]
    parts = cast(jnp.concatenate(split3(from_owner), axis=0))
    total = jnp.zeros((CS, 96), F32)
    for b in range(FACES // FB):
        cols = slice(FB * b, FB * (b + 1))
        hot = jnp.where(iota((DEV, FB), 0) == owner[:, cols], 1.0, 0.0)
        y = dot_nn(parts, cast(hot))
        y = y[0:32, :] + y[32:64, :] + y[64:96, :]
        which = iota((CAP, FB), 0) == rank[:, cols]
        v0 = jnp.sum(jnp.where(which, y[0:16, :], 0.0), axis=0, keepdims=True)
        km = jnp.sum(jnp.where(which, y[16:32, :], 0.0), axis=0, keepdims=True)
        kf = coef[0:1, cols]
        p = top[:, cols]
        tw = (kf * p + km * v0) / (kf * (1.0 - corner_f) + km * (1.0 - corner_m))
        heat = kf * (p + (corner_f - 1.0) * tw)
        span_hot, pitch_hot = cell_tables(cell[:, cols])
        pieces = [jnp.where(pitch_hot, part, 0.0) for part in split3(heat)]
        total = total + dot_nt(cast(span_hot), cast(jnp.concatenate(pieces, axis=0)))
    wall = -0.5 * (total[:, 0:32] + total[:, 32:64] + total[:, 64:96])
    wall = jnp.concatenate([wall, jnp.zeros((CS, 96), F32)], axis=1)
    first_lane = iota((CS, 128), 1) == 0
    copies = []
    for p in range(CP):
        column = wall if p == 0 else pltpu.roll(wall, 128 - p, 1)
        kept[p] = kept[p] + jnp.where(first_lane, column, 0.0)
        if p % 16 == 15:
            planes = pl.ds(p - 15, 16)
            copies.append(
                pltpu.make_async_copy(
                    kept.at[planes], out.at[2, planes, :, pl.ds(0, 128)], sems.at[len(copies)]
                )
            )
            copies[-1].start()

    own = send[...]
    lane = iota((DEV, 128), 1)
    kf = pltpu.roll(got, 96, 1)
    p = pltpu.roll(got, 80, 1)
    km = pltpu.roll(own, 112, 1)
    valid = lane < CAP
    tw = (kf * p + km * own) / jnp.where(valid, kf * (1.0 - corner_f) + km * (1.0 - corner_m), 1.0)
    tw = jnp.where(valid, tw, 0.0)
    used = jnp.where(jnp.logical_and(valid, kf > 0.0), 1.0, 0.0)
    for step in (16, 32, 64):
        tw = tw + pltpu.roll(tw, step, 1)
        used = used + pltpu.roll(used, step, 1)
    mine = (lane >> 4) == (iota((DEV, 128), 0) & 7)
    tw = jnp.where(mine, tw, 0.0)
    used = jnp.where(mine, used, 0.0)
    gain = 0.5 * metal_inv[:, 0:1]
    for g in range(16):
        rows = slice(8 * g, 8 * g + 8)
        cols = slice(128 * g, 128 * g + 128)
        tw_row = jnp.sum(tw[rows, :], axis=0, keepdims=True)
        used_row = jnp.sum(used[rows, :], axis=0, keepdims=True)
        metal_out[:, cols] = jnp.where(
            used_row > 0.5, free[:, cols] + gain * tw_row, metal[:, cols]
        )
    copies.append(pltpu.make_async_copy(metal_out, metal_give, sems.at[2]))
    copies[-1].start()
    for copy in copies:
        copy.wait()


def spec(space):
    return pl.BlockSpec(memory_space=space)


ANY = pl.ANY
VM = pltpu.VMEM
HBM = pltpu.HBM


def shape(dims, dtype=F32):
    return jax.ShapeDtypeStruct(dims, dtype)


def params(limit=VMEM_LIMIT):
    return pltpu.CompilerParams(vmem_limit_bytes=limit)


def cost(microseconds):
    return pl.CostEstimate(
        flops=0, bytes_accessed=int(microseconds * 3_000_000), transcendentals=0
    )


def local(
    flow_state,
    wall_inverse,
    metal_inverse,
    metal_state,
    metal_conduct,
    face_coef,
    owner_map,
    face_cell,
    sample_col,
    sample_low,
):
    owner = owner_map.reshape(1, FACES)
    cell = face_cell.reshape(1, FACES)
    low = sample_low.reshape(1, FACES)
    conduct = metal_conduct.reshape(16, 128)
    send, give_pa, give_pb, give_sa, give_sb, rank, top, free, force = pl.pallas_call(
        first_kernel,
        name="first",
        in_specs=[spec(HBM)] * 10,
        out_specs=[spec(HBM)] * 5 + [spec(VM)] * 3 + [spec(HBM)],
        out_shape=[
            shape((DEV, 128)),
            shape((4, CS, GN)),
            shape((4, CS, GN)),
            shape((4, CP, GN)),
            shape((4, CP, GN)),
            shape((1, FACES), I32),
            shape((1, FACES)),
            shape((MP, SLOT_DEV)),
            shape((ROOM, FACES, 128)),
        ],
        scratch_shapes=[
            pltpu.VMEM((8, COLS + PAD, 128), F32),
            pltpu.VMEM((FACES, 128), I32),
            pltpu.VMEM((FACES, 128), F32),
            pltpu.VMEM((FACES, 128), F32),
            pltpu.VMEM((DEV, 128), F32),
            pltpu.VMEM((2, 4, CS, GN), F32),
            pltpu.VMEM((2, 4, CP, GN), F32),
            pltpu.SemaphoreType.DMA((12,)),
            pltpu.SMEM((FACES,), I32),
            pltpu.VMEM((1, FACES), I32),
            pltpu.VMEM((1, FACES), I32),
            pltpu.VMEM((2, FACES), F32),
            pltpu.VMEM((1, FACES), I32),
            pltpu.VMEM((WM, WM), F32),
            pltpu.VMEM((MP, MP), F32),
            pltpu.VMEM((MP, SLOT_DEV), F32),
            pltpu.VMEM((16, 128), F32),
        ],
        compiler_params=params(VMEM_WHOLE),
        cost_estimate=cost(7),
    )(
        flow_state, sample_col, low, owner, face_coef, cell, wall_inverse, metal_inverse,
        metal_state, conduct,
    )

    recv = lax.all_to_all(send, AXES, split_axis=0, concat_axis=0, tiled=True)

    n_pitch, n_span = lax.axis_size("pitch"), lax.axis_size("span")
    within_p = [(i, i ^ 1) for i in range(n_pitch)]
    across_p = [(i, (i + (1 if i & 1 else -1)) % n_pitch) for i in range(n_pitch)]
    within_s = [(i, i ^ 1) for i in range(n_span)]
    across_s = [(i, i + (1 if i & 1 else -1)) for i in range(1, n_span - 1)]
    got_pa = lax.ppermute(give_pa, "pitch", within_p)
    got_pb = lax.ppermute(give_pb, "pitch", across_p)
    got_sa = lax.ppermute(give_sa, "span", within_s)
    got_sb = lax.ppermute(give_sb, "span", across_s)

    new_state, kept = pl.pallas_call(
        stencil_kernel,
        name="stencil",
        in_specs=[spec(ANY), spec(ANY)] + [spec(VM)] * 3 + [spec(ANY)] * 2 + [spec(VM)] * 2,
        out_specs=[spec(ANY), spec(VM)],
        out_shape=[shape((4, CP, CS, GN)), shape((CP, CS, 128))],
        scratch_shapes=[
            pltpu.VMEM((2, 4, CP + 2, ROWS, 128), F32),
            pltpu.VMEM((2, 4, CP, CS, 128), F32),
            pltpu.VMEM((FACES, 128), F32),
            pltpu.VMEM((CS, 128), F32),
            pltpu.VMEM((GROUP * CS, GN), F32),
            pltpu.VMEM((GROUP * CS, GN), F32),
            pltpu.SemaphoreType.DMA((10,)),
        ],
        compiler_params=params(),
        cost_estimate=cost(10),
    )(flow_state, force, face_coef, cell, wall_inverse, got_pa, got_pb, got_sa, got_sb)

    new_state, metal_out = pl.pallas_call(
        last_kernel,
        name="last",
        in_specs=[spec(ANY)] + [spec(VM)] * 12,
        out_specs=[spec(ANY), spec(HBM)],
        out_shape=[shape((4, CP, CS, GN)), shape((MP, SLOT_DEV))],
        input_output_aliases={0: 0},
        scratch_shapes=[pltpu.VMEM((MP, SLOT_DEV), F32), pltpu.SemaphoreType.DMA((3,))],
        compiler_params=params(),
        cost_estimate=cost(3),
    )(
        new_state, kept, recv, send, free, metal_state, owner, rank, top, face_coef, cell,
        wall_inverse, metal_inverse,
    )
    return (new_state, metal_out)


def solution(mesh):
    return jax.shard_map(
        local,
        mesh=mesh,
        in_specs=(
            P(None, "pitch", "span", None),
            P(),
            P(),
            P(None, ("pitch", "span")),
            P(("pitch", "span")),
            P(None, ("pitch", "span")),
            P(("pitch", "span"), None),
            P(("pitch", "span")),
            P(("pitch", "span")),
            P(("pitch", "span")),
        ),
        out_specs=(P(None, "pitch", "span", None), P(None, ("pitch", "span"))),
        check_vma=False,
    )
```
